32 devices in a mesh: fsdp: 4 (over y, core), seq: 8 (over z, x).
Axes of the slice: x: 2, y: 2, z: 4, core: 2. Of those that a mesh axis runs over, the one named last changes fastest.
Arguments:
- tokens: bfloat16 [3, 4, 1024, 1024], P(None, 'fsdp', 'seq'), may hold values from -6 to 6
- scene_ids: int32 [3, 4, 1024], P(None, 'fsdp'), may hold values from 0 to 4, as said below
- valid_mask: int32 [3, 4, 1024], P(None, 'fsdp'), may hold values 0 or 1
- norm_gain: bfloat16 [1024], P(('fsdp', 'seq')), may hold values from 0.099609375 to 1.8984375
- w_in: bfloat16 [1024, 4384], P(('fsdp', 'seq')), may hold values from -0.1875 to 0.1875
- conv_w: bfloat16 [4, 2304], P(None, ('fsdp', 'seq')), may hold values from -3 to 3
- conv_b: bfloat16 [2304], P(('fsdp', 'seq')), may hold values from -0.5 to 0.5
- dt_bias: float32 [32], P('seq'), may hold values from -5 to -1
- a_log: float32 [32], P('seq'), may hold values from -7 to 1
- d_skip: float32 [32], P('seq'), may hold values from 0.5 to 1.5
- gate_gain: bfloat16 [2048], P(('fsdp', 'seq')), may hold values from 0.099609375 to 1.8984375
- w_out: bfloat16 [2048, 1024], P(('fsdp', 'seq')), may hold values from -0.125 to 0.125
- d_out: bfloat16 [3, 4, 1024, 1024], P(None, 'fsdp', 'seq'), may hold values from -6 to 6
Outputs:
- block_out: bfloat16 [3, 4, 1024, 1024], P(None, 'fsdp', 'seq')
- grad_in: bfloat16 [3, 4, 1024, 1024], P(None, 'fsdp', 'seq')
- grad_norm_gain: float32 [1024], P(('fsdp', 'seq'))
- grad_w_in: float32 [1024, 4384], P(('fsdp', 'seq'))
- grad_conv_w: float32 [4, 2304], P(None, ('fsdp', 'seq'))
- grad_conv_b: float32 [2304], P(('fsdp', 'seq'))
- grad_dt_bias: float32 [32], P('seq')
- grad_a_log: float32 [32], P('seq')
- grad_d_skip: float32 [32], P('seq')
- grad_gate_gain: float32 [2048], P(('fsdp', 'seq'))
- grad_w_out: float32 [2048, 1024], P(('fsdp', 'seq'))
The draws below stay inside these ranges and needn't reach their ends.
Inputs may be any that keep to these rules, and one draw needn't show every extreme that they name: `scene_ids`: in each packed sequence scene numbers start at 0 and rise by one at each of four scene starts. Counting positions from 0: scene 1 starts at a position of 1 or more, before scene 2; scene 2 starts at a position from 2 to 64; scene 3 starts at a position from 960 to 1022; scene 4 starts after scene 3, at 1023 at the latest.
All inputs are finite; a program needn't handle non-finite values. No bound on the sum of `valid_mask` on one device may be relied on, other than what follows from the above.
Results may differ from the reference program's by a relative error of at most 0.013.
Values may be sent and summed in bfloat16 or wider, within the bound.
No kernel may reach another device: no remote copies, remote signals or barrier semaphores. Data moves between devices by JAX's collectives and lax.ppermute only.
A program may use at most 192 MiB of HBM per device.

```python
import jax
import jax.numpy as jnp
from jax import lax

D = 1024
H = 32
P_SIZE = 64
N = 128
KERNEL = 4
SPAN = 256
MB = 3
TOK_DEV = 128
GROUPS = 4
LEN = 1024


def draw_scene_ids(key, part):
    key = jax.random.fold_in(key, 11)
    row_count = MB * GROUPS
    subkeys = jax.random.split(key, 4)
    half_dev = TOK_DEV // 2
    start_big = jax.random.randint(subkeys[0], (row_count, 1), 2, half_dev + 1)
    start_small = jax.random.randint(subkeys[1], (row_count, 1), 1, start_big)
    end_big = jax.random.randint(subkeys[2], (row_count, 1), LEN - half_dev, LEN - 1)
    end_last = jax.random.randint(subkeys[3], (row_count, 1), end_big + 1, LEN)
    position = jnp.arange(LEN, dtype=jnp.int32)[None, :]
    scene = (position >= start_small).astype(jnp.int32) + (position >= start_big).astype(jnp.int32) + (position >= end_big).astype(jnp.int32) + (position >= end_last).astype(jnp.int32)
    return scene.reshape(MB, GROUPS, LEN)


def touch_ends(entries, rng, least, top_value):
    longest = entries.shape.index(max(entries.shape))
    spots = []
    for shift in (0, 1):
        where = [jax.random.randint(jax.random.fold_in(rng, axis), (), 0, length) for axis, length in enumerate(entries.shape)]
        where[longest] = (where[longest] + shift) % entries.shape[longest]
        spots.append(tuple(where))
    return entries.at[spots[0]].set(least).at[spots[1]].set(top_value)


def level_of(rng, shape, pieces, smallest, top_value):
    loudness = 1.0
    for dim, blocks in pieces:
        steps = jax.random.uniform(jax.random.fold_in(jax.random.fold_in(rng, 6), dim), (blocks,), jnp.float32, smallest / len(pieces), top_value / len(pieces))
        loudness = loudness * jnp.repeat(jnp.exp(steps), shape[dim] // blocks).reshape((-1,) + (1,) * (len(shape) - 1 - dim))
    return loudness


def gaussian(key, extent, deviation, reach, cuts=(), held_as=jnp.bfloat16):
    entries = deviation * jax.random.normal(key, extent, jnp.float32)
    if cuts:
        entries = entries * level_of(key, extent, cuts, -0.22, 0.18)
    return jnp.clip(entries, -reach, reach).astype(held_as)


def setup_inputs(seed: int = 0) -> dict:
    streams_of = jax.random.split(jax.random.key(seed), 14)
    tokens = gaussian(streams_of[0], (MB, GROUPS, LEN, D), 1.0, 6.0, ((1, 4), (2, 8)))
    scene_ids = draw_scene_ids(jax.random.fold_in(streams_of[13], 71), 0)
    valid_mask = touch_ends((jax.random.randint(streams_of[2], (MB, GROUPS, LEN), 0, 8) < 7).astype(jnp.int32), jax.random.fold_in(streams_of[2], 1), 0, 1)
    norm_gain = jnp.clip(1.0 + 0.18 * jax.random.normal(streams_of[3], (D,), jnp.float32), 0.099609375, 1.8984375).astype(jnp.bfloat16)
    w_in = gaussian(streams_of[4], (D, 2 * H * P_SIZE + 2 * N + H), D ** -0.5, 0.1875, ((0, 32),))
    conv_w = gaussian(streams_of[5], (KERNEL, H * P_SIZE + 2 * N), KERNEL ** -0.5, 3.0, ((1, 32),))
    conv_b = jnp.clip(jax.random.uniform(streams_of[6], (H * P_SIZE + 2 * N,), jnp.float32, -0.5, 0.5) * level_of(streams_of[6], (H * P_SIZE + 2 * N,), ((0, 32),), -0.4, 0.0), -0.5, 0.5).astype(jnp.bfloat16)
    dt_bias = jnp.clip(-5.0 + 4.0 * jax.random.uniform(streams_of[7], (H,), jnp.float32) ** level_of(streams_of[7], (H,), ((0, 8),), -0.2, 0.2), -5.0, -1.0)
    a_log = jnp.clip(-7.0 + 8.0 * jax.random.uniform(streams_of[8], (H,), jnp.float32) ** level_of(streams_of[8], (H,), ((0, 8),), -0.2, 0.2), -7.0, 1.0)
    d_skip = jnp.clip(0.5 + 1.0 * jax.random.uniform(streams_of[9], (H,), jnp.float32) ** level_of(streams_of[9], (H,), ((0, 8),), -0.2, 0.2), 0.5, 1.5)
    gate_gain = jnp.clip(1.0 + 0.18 * jax.random.normal(streams_of[10], (H * P_SIZE,), jnp.float32), 0.099609375, 1.8984375).astype(jnp.bfloat16)
    w_out = gaussian(streams_of[11], (H * P_SIZE, D), (H * P_SIZE) ** -0.5, 0.125, ((0, 32),))
    d_out = gaussian(streams_of[12], (MB, GROUPS, LEN, D), 1.0, 6.0, ((1, 4), (2, 8)))
    return dict(tokens=tokens, scene_ids=scene_ids, valid_mask=valid_mask, norm_gain=norm_gain, w_in=w_in, conv_w=conv_w, conv_b=conv_b, dt_bias=dt_bias, a_log=a_log, d_skip=d_skip, gate_gain=gate_gain, w_out=w_out, d_out=d_out)


epsilon = 1e-05

@jax.custom_vjp
def low(v):
    return lax.optimization_barrier(v.astype(jnp.bfloat16)).astype(jnp.float32)

@jax.custom_vjp
def low_back(v):
    return v

def low_keep(v):
    return (low(v), None)

def low_pass(kept, grad):
    return (grad,)

def back_keep(v):
    return (v, None)

def back_low(kept, grad):
    return (low(grad),)
low.defvjp(low_keep, low_pass)
low_back.defvjp(back_keep, back_low)

def causal_conv(extended, ext_ids, conv_kernel, conv_bias):
    length = extended.shape[0] - KERNEL + 1
    own_ids = ext_ids[KERNEL - 1:]
    summed = jnp.zeros((length, extended.shape[1]), jnp.float32) + conv_bias
    for offset in range(KERNEL):
        same_scene = (ext_ids[offset:offset + length] == own_ids).astype(jnp.float32)
        summed = summed + conv_kernel[offset] * extended[offset:offset + length] * same_scene[:, None]
    return summed

def state_scan(values, b_part, c_part, step_size, a_log, d_skip, scene_row):
    length, head_count, head_dim = values.shape
    state_dim = b_part.shape[1]
    blocks = length // SPAN
    decay_rate = jnp.exp(a_log)
    block_ids = scene_row.reshape(blocks, SPAN)
    before = jnp.concatenate([jnp.full((1,), -1, jnp.int32), block_ids[:-1, -1]])
    lower_mask = lax.broadcasted_iota(jnp.int32, (SPAN, SPAN), 0) >= lax.broadcasted_iota(jnp.int32, (SPAN, SPAN), 1)
    highest = lax.Precision.HIGHEST

    def span_step(carried, span_item):
        span_x, span_b, span_c, span_dt, span_ids, prior_id = span_item
        log_decay = -span_dt * decay_rate
        cumulative = jnp.cumsum(log_decay, axis=0).T
        same_scene = lower_mask & (span_ids[:, None] == span_ids[None, :])
        log_ratio = cumulative[:, :, None] - cumulative[:, None, :]
        decay_in = jnp.exp(jnp.where(same_scene[None], log_ratio, -jnp.inf))
        intersection = jnp.dot(span_c, span_b.T, precision=highest)
        scaled = span_x * span_dt[:, :, None]
        inside = jnp.einsum('hts,shp->thp', decay_in * intersection[None], scaled, precision=highest)
        carry_in = (span_ids == prior_id).astype(jnp.float32)
        reach_in = jnp.exp(cumulative) * carry_in[None, :]
        from_state = jnp.einsum('tn,hpn->thp', span_c, carried, precision=highest) * reach_in.T[:, :, None]
        tail_mask = span_ids == span_ids[-1]
        weight_end = jnp.exp(jnp.where(tail_mask[None, :], cumulative[:, -1:] - cumulative, -jnp.inf))
        fresh_state = jnp.einsum('hs,shp,sn->hpn', weight_end, scaled, span_b, precision=highest)
        carried = carried * (jnp.exp(cumulative[:, -1]) * carry_in[-1])[:, None, None] + fresh_state
        block_out = inside + from_state + d_skip[None, :, None] * span_x
        return (carried, block_out)
    initial = jnp.zeros((head_count, head_dim, state_dim), jnp.float32)
    _, outputs = lax.scan(jax.checkpoint(span_step), initial, (values.reshape(blocks, SPAN, head_count, head_dim), b_part.reshape(blocks, SPAN, state_dim), c_part.reshape(blocks, SPAN, state_dim), step_size.reshape(blocks, SPAN, head_count), block_ids, before))
    return outputs.reshape(length, head_count, head_dim)

def mixer_block(inputs, norm_gain, w_in, conv_w, conv_b, dt_bias, a_log, d_skip, gate_gain, w_out, scene_row, valid_row):
    highest = lax.Precision.HIGHEST
    length = inputs.shape[0]
    inner_width = H * P_SIZE
    in_scale = lax.rsqrt(lax.optimization_barrier(jnp.mean(inputs * inputs, axis=-1, keepdims=True)) + epsilon)
    normed = low(inputs * in_scale * norm_gain)
    projected = low_back(jnp.dot(normed, w_in, precision=highest))
    gate_in = projected[:, :inner_width]
    conv_in = projected[:, inner_width:2 * inner_width + 2 * N]
    step_raw = projected[:, 2 * inner_width + 2 * N:]
    extended = jnp.concatenate([jnp.zeros((KERNEL - 1, conv_in.shape[1]), jnp.float32), conv_in], axis=0)
    ext_ids = jnp.concatenate([jnp.full((KERNEL - 1,), -1, jnp.int32), scene_row])
    conv_pre = causal_conv(extended, ext_ids, conv_w, conv_b)
    activated = jax.nn.silu(conv_pre)
    x_part = low_back(low(activated[:, :inner_width]))
    b_part = low(activated[:, inner_width:inner_width + N])
    c_part = low(activated[:, inner_width + N:])
    step_in = low_back(low(step_raw))
    step_size = jax.nn.softplus(step_in + dt_bias) * valid_row[:, None]
    scanned = state_scan(x_part.reshape(length, H, P_SIZE), b_part, c_part, step_size, a_log, d_skip, scene_row)
    mixed_out = low_back(low(scanned.reshape(length, inner_width)))
    gated_out = mixed_out * jax.nn.silu(gate_in)
    out_scale = lax.rsqrt(lax.optimization_barrier(jnp.mean(gated_out * gated_out, axis=-1, keepdims=True)) + epsilon)
    normed_out = low(gated_out * out_scale * gate_gain)
    return inputs + jnp.dot(normed_out, w_out, precision=highest)

def reference(tokens, scene_ids, valid_mask, norm_gain, w_in, conv_w, conv_b, dt_bias, a_log, d_skip, gate_gain, w_out, d_out):
    params = tuple((weight.astype(jnp.float32) for weight in (norm_gain, w_in, conv_w, conv_b, dt_bias, a_log, d_skip, gate_gain, w_out)))
    seq_total = MB * GROUPS

    def one_seq(totals, seq_item):
        seq_in, seq_ids, seq_mask, seq_grad = seq_item

        def forward(inputs, *weight_list):
            return mixer_block(inputs, *weight_list, seq_ids, seq_mask.astype(jnp.float32))
        result, pullback = jax.vjp(forward, seq_in.astype(jnp.float32), *params)
        grad_list = pullback(seq_grad.astype(jnp.float32))
        totals = jax.tree.map(jnp.add, totals, tuple(grad_list[1:]))
        return (totals, (result.astype(jnp.bfloat16), grad_list[0].astype(jnp.bfloat16)))
    zero_grads = tuple((jnp.zeros_like(weight) for weight in params))
    totals, (results, input_grads) = lax.scan(one_seq, zero_grads, (tokens.reshape(seq_total, LEN, D), scene_ids.reshape(seq_total, LEN), valid_mask.reshape(seq_total, LEN), d_out.reshape(seq_total, LEN, D)))
    g_norm, g_win, g_convw, g_convb, g_dtbias, g_alog, g_dskip, g_gate, g_wout = totals
    return (results.reshape(MB, GROUPS, LEN, D), input_grads.reshape(MB, GROUPS, LEN, D), g_norm, g_win, g_convw, g_convb, g_dtbias, g_alog, g_dskip, g_gate, g_wout)
```

```python
import functools

import numpy as np
import jax
import jax.numpy as jnp
from jax import lax
from jax.experimental import pallas as pl
from jax.experimental.pallas import tpu as pltpu
from jax.sharding import PartitionSpec as P

D = 1024
H = 32
P_SIZE = 64
N = 128
KERNEL = 4
MB = 3
INNER = H * P_SIZE
CONV = INNER + 2 * N
HALO = 16
FRONT = 384
TILE = 256
P_TILES = 3
P_COLS = FRONT + P_TILES * TILE
W1_COLS = FRONT + INNER
Q_COLS = W1_COLS - P_COLS
GROUP = 8
EPS = 1e-05
F32 = jnp.float32
BF16 = jnp.bfloat16
BOTH = ("fsdp", "seq")
VMEM = pl.BlockSpec(memory_space=pltpu.VMEM)
SMEM = pl.BlockSpec(memory_space=pltpu.SMEM)
ANY = pl.BlockSpec(memory_space=pl.ANY)
HBM = pl.BlockSpec(memory_space=pltpu.HBM)
SMALL = pl.CostEstimate(flops=1, bytes_accessed=1, transcendentals=0)


def shape(dims, dtype=F32):
    return jax.ShapeDtypeStruct(dims, dtype)


def params(mib=48):
    return pltpu.CompilerParams(vmem_limit_bytes=mib * 2**20)


def permute(block, mask):
    size = lax.axis_size("fsdp") * lax.axis_size("seq")
    return lax.ppermute(block, BOTH, [(i, i ^ mask) for i in range(size)])


def tied(*values):
    return lax.optimization_barrier(values)


def combos(masks):
    found = [0]
    for mask in masks:
        found += [c | mask for c in found]
    return found[1:]


def spread(held, stage):
    return jnp.concatenate([held] + [permute(held, m) for m in stage], axis=0)


def cut(total, stage):
    width = total.shape[0] // (len(stage) + 1)
    return [total[i * width : (i + 1) * width] for i in range(len(stage) + 1)]


def fold(pieces, stage, dtype=BF16):
    total = pieces[0].astype(F32)
    for part, m in zip(pieces[1:], stage):
        total = total + permute(part, m).astype(F32)
    return total.astype(dtype)


def order_of(stages):
    masks = [0]
    for stage in stages:
        held = list(masks)
        for m in stage:
            masks += [k ^ m for k in held]
    return np.array(masks, np.int32)


def split3(v):
    high = lax.reduce_precision(v, 8, 7)
    mid = lax.reduce_precision(v - high, 8, 7)
    return [p.astype(BF16) for p in (high, mid, v - high - mid)]


def nn(a, b):
    return jnp.dot(a, b, preferred_element_type=F32)


def nt(a, b):
    return lax.dot_general(a, b, (((1,), (1,)), ((), ())), preferred_element_type=F32)


def tn(a, b):
    return lax.dot_general(a, b, (((0,), (0,)), ((), ())), preferred_element_type=F32)


def split(v, count=3):
    parts = []
    for _ in range(count):
        part = v.astype(BF16)
        parts.append(part)
        v = v - part.astype(F32)
    return parts


def one_hot(tile):
    row = lax.broadcasted_iota(jnp.int32, (N, TILE), 0)
    col = lax.broadcasted_iota(jnp.int32, (N, TILE), 1)
    return ((row % H == tile * (TILE // P_SIZE) + col // P_SIZE) & (row < 3 * H)).astype(F32).astype(BF16)


def packed(v):
    lane = lax.broadcasted_iota(jnp.int32, v.shape, 1)
    v = jnp.where(lane < H, v, 0.0)
    high, mid, low = [p.astype(F32) for p in split(v)]
    return (high + pltpu.roll(mid, H, 1) + pltpu.roll(low, 2 * H, 1)).astype(BF16)


def wide(parts, hot):
    return nn(parts, hot)


def head_sum(v, hot):
    return sum(nt(p, hot) for p in split(v, 2))


def sigmoid(v):
    return 1.0 / (1.0 + jnp.exp(-v))


def exact_sum(matrix, v):
    return sum(nn(matrix, p) for p in split(v))


def turned(v):
    return v.astype(F32).T


def block_copies(lin, masks, sources, place, sems):
    copies = []
    half = len(masks) // 2
    for r, mask in enumerate(masks):
        where = lin ^ int(mask)
        source = sources[r // half].at[r % half]
        for src, dst in place(source, where):
            copy = pltpu.make_async_copy(src, dst, sems.at[len(copies)])
            copy.start()
            copies.append(copy)
    return copies


def rows_at(ref, where, height, cols):
    return ref.at[pl.ds(pl.multiple_of(where * height, height), height), cols]


def put(out_ref, piece, offset, width, rows):
    first, shift = offset // 128, offset % 128
    lane = lax.broadcasted_iota(jnp.int32, piece.shape, 1)
    moved = pltpu.roll(jnp.where(lane < width, piece, 0.0), shift, 1) if shift else jnp.where(lane < width, piece, 0.0)
    if shift + width > 128:
        out_ref[rows, first * 128 : first * 128 + 128] += jnp.where(lane >= shift, moved, 0.0)
        out_ref[rows, first * 128 + 128 : first * 128 + 256] += jnp.where(lane < shift, moved, 0.0)
    else:
        out_ref[rows, first * 128 : first * 128 + 128] += moved


def get(in_ref, offset, width, rows):
    first, shift = offset // 128, offset % 128
    piece = in_ref[rows, first * 128 : first * 128 + 128]
    lane = lax.broadcasted_iota(jnp.int32, piece.shape, 1)
    if shift + width > 128:
        piece = jnp.where(lane >= shift, piece, in_ref[rows, first * 128 + 128 : first * 128 + 256])
    piece = pltpu.roll(piece, 128 - shift, 1) if shift else piece
    return jnp.where(lane < width, piece, 0.0)


def small_kernel(n_dev, n_s, total, part, tab, small_ref, line_ref, taps_ref, gin_ref, gout_ref, hp_ref, skip_ref, meta_ref, col_ref, row_ref, conv_s):
    conv_s[...] = jnp.zeros_like(conv_s)
    gin_ref[...] = jnp.zeros_like(gin_ref)
    gout_ref[...] = jnp.zeros_like(gout_ref)
    hp_ref[...] = jnp.zeros_like(hp_ref)
    channels, features, wider, heads = CONV // n_dev, D // n_dev, INNER // n_dev, H // n_s
    everything = slice(0, 8)
    for d in range(n_dev):
        block = small_ref[tab[d]]
        if part:
            block = block.astype(F32)
            block = pltpu.roll(block[:8] + block[8:16] + block[16:24], 128 - H, 1)
        put(conv_s, block, d * channels, channels, everything)
        put(gin_ref, block[5:6], d * features, features, slice(0, 1))
        put(gout_ref, block[6:7], d * wider, wider, slice(0, 1))
        if d < n_s:
            for k in range(3):
                head = block[7:8] if k == 0 else pltpu.roll(block[7:8], 128 - k * heads, 1)
                put(hp_ref, head, d * heads, heads, slice(k, k + 1))
    taps_ref[:, : 2 * N] = conv_s[:, INNER:]
    taps_ref[:, 2 * N :] = conv_s[:, :INNER]
    lane = lax.broadcasted_iota(jnp.int32, (1, N), 1)
    hp_ref[1:2, :] = jnp.where(lane < H, jnp.exp(hp_ref[1:2, :]), 0.0)
    parts = packed(jnp.broadcast_to(hp_ref[2:3, :], (16, N)))
    for j in range(INNER // TILE):
        skip_ref[:, j * TILE : (j + 1) * TILE] = wide(parts, one_hot(j))[:1]
    line = line_ref[...]
    wide_line = line.shape[1]
    moved = lambda v, k: pltpu.roll(v, wide_line - k, 1)[:, :total]
    ids = line[0:1]
    own = moved(ids, HALO)
    keep = lambda test: jnp.where(test, 1.0, 0.0)
    same = [keep(moved(ids, HALO - 3 + k) == own) for k in range(3)]
    before = jnp.sum(jnp.where(lax.broadcasted_iota(jnp.int32, ids.shape, 1) == HALO - 1, ids, 0.0), axis=1, keepdims=True)
    final = jnp.sum(jnp.where(lax.broadcasted_iota(jnp.int32, ids.shape, 1) == HALO + total - 1, ids, 0.0), axis=1, keepdims=True)
    rows = same + [moved(line[1:2], HALO), keep(own == before), keep(own == final), own, own]
    turned_rows = jnp.concatenate(rows, axis=0).T
    meta_ref[...] = turned_rows
    col_ref[...] = turned_rows[:, 6:7]
    row_ref[...] = own


def small_stage(tab, small, line, n_dev, n_s, total):
    return pl.pallas_call(
        functools.partial(small_kernel, n_dev, n_s, total, small.dtype == BF16),
        out_shape=(
            shape((8, CONV)), shape((1, D)), shape((1, INNER)), shape((8, N)), shape((1, INNER)), shape((total, 8)), shape((total, 1)), shape((1, total)),
        ),
        in_specs=[SMEM, VMEM, VMEM],
        out_specs=tuple([VMEM] * 8),
        scratch_shapes=[pltpu.VMEM((8, CONV), F32)],
        compiler_params=params(),
        cost_estimate=SMALL,
        name="small_stage",
    )(tab, small, line)


def grad_small(n_dev, n_s, tab, gp_ref, gq_ref, gout_ref, few_ref, out_ref, conv_s):
    split_at = P_TILES * TILE
    conv_s[:, :split_at] = gp_ref[:, FRONT:]
    conv_s[:, split_at:INNER] = gq_ref[...]
    conv_s[:, INNER:] = gp_ref[:, 128:FRONT]
    channels, wider, heads = CONV // n_dev, INNER // n_dev, H // n_s
    for d in range(n_dev):
        where = (d % n_s) * heads
        head = jnp.zeros((1, 128), F32)
        for k in range(3):
            piece = get(few_ref.at[k], where, heads, slice(0, 1))
            head = head + (pltpu.roll(piece, k * heads, 1) if k else piece)
        rows = [get(conv_s, d * channels, channels, slice(0, 8))[:5], jnp.zeros((1, 128), F32)]
        rows += [get(gout_ref, d * wider, wider, slice(0, 1)), head]
        out_ref[tab[d]] = jnp.concatenate(rows, axis=0)


def grad_small_stage(tab, gp, gq, gout, few, n_dev, n_s):
    return pl.pallas_call(
        functools.partial(grad_small, n_dev, n_s),
        out_shape=shape((n_dev, 8, 128)),
        in_specs=[SMEM] + [VMEM] * 4,
        out_specs=VMEM,
        scratch_shapes=[pltpu.VMEM((8, CONV), F32)],
        compiler_params=params(),
        cost_estimate=SMALL,
        name="grad_small_stage",
    )(tab, gp, gq, gout, few)


def first_kernel(masks_p, masks_q, total, lin_ref, halo_ref, t0_ref, t1_ref, t2_ref, gain_ref, meta_ref, taps_ref, hp_ref, po, px, qo, qx,
                 w1_ref, normed_ref, cin_ref, pre_ref, bc_ref, x_ref, dtx_ref, hd_ref, cumt_ref, pay_ref, cin_s, w1_s, cin_b, pre_b, sem_p, sem_q, sem_out):
    lin = lin_ref[0]
    rows = D // len(masks_p)
    place = lambda cols: lambda src, where: [(src, rows_at(w1_s, where, rows, cols))]
    first = block_copies(lin, masks_p, (po, px), place(pl.ds(0, P_COLS)), sem_p)
    second = block_copies(lin, masks_q, (qo, qx), place(pl.ds(P_COLS, Q_COLS)), sem_q)
    start = 0
    for ref in (halo_ref, t0_ref, t1_ref, t2_ref):
        u = ref[...].astype(F32)
        scale = lax.rsqrt(jnp.mean(u * u, axis=-1, keepdims=True) + EPS)
        normed_ref[start : start + u.shape[0], :] = (u * scale * gain_ref[...]).astype(BF16)
        start += u.shape[0]
    written = []

    def write(source, target):
        copy = pltpu.make_async_copy(source, target, sem_out.at[len(written)])
        copy.start()
        written.append(copy)

    for copy in first:
        copy.wait()
    meta = meta_ref[...]
    same = [meta[:, k : k + 1] for k in range(3)]
    valid, carry, tail = meta[:, 3:4], meta[:, 4:5], meta[:, 5:6]

    def conv(made, cols):
        cin_s[...] = made
        cin_b[:, cols] = made.astype(BF16)
        acc = taps_ref[4:5, cols] + taps_ref[3:4, cols] * made[HALO:]
        for k in range(3):
            acc = acc + taps_ref[k : k + 1, cols] * (cin_s[HALO - 3 + k : HALO - 3 + k + total, :] * same[k])
        pre_b[:, cols] = acc.astype(BF16)
        write(cin_b.at[:, cols], cin_ref.at[:, cols])
        write(pre_b.at[:, cols], pre_ref.at[:, cols])
        return (acc * sigmoid(acc)).astype(BF16)

    front = nn(normed_ref[...], w1_s[:, :FRONT])
    lane = lax.broadcasted_iota(jnp.int32, (total, 128), 1)
    shifted = jnp.where(lane < H, front[HALO:, :128], 0.0).astype(BF16).astype(F32) + hp_ref[0:1, :]
    dt = (jnp.maximum(shifted, 0.0) + jnp.log1p(jnp.exp(-jnp.abs(shifted)))) * valid
    row = lax.broadcasted_iota(jnp.int32, (total, total), 0)
    col = lax.broadcasted_iota(jnp.int32, (total, total), 1)
    lower = (row >= col).astype(F32).astype(BF16)
    cum = exact_sum(lower, -dt * hp_ref[1:2, :])
    reach = jnp.exp(cum) * carry
    w_end = jnp.exp(cum[total - 1 : total] - cum) * tail
    hd_ref[0], hd_ref[1], hd_ref[2], hd_ref[3], hd_ref[4] = dt, cum, reach, w_end, shifted
    cumt_ref[...] = cum.T[:H]
    bc = conv(front[:, 128:], pl.ds(0, 2 * N))
    bc_ref[...] = bc
    b_turned = turned(bc[:, :N]).astype(BF16)
    through = jnp.broadcast_to(reach[total - 1 : total], (8, N))
    dt_parts, both_parts = packed(dt), packed(dt * w_end)
    through_parts = [packed(p.astype(F32)) for p in split(through)]
    for j in range(INNER // TILE):
        if j == P_TILES:
            for copy in second:
                copy.wait()
            write(w1_s, w1_ref)
        cols = pl.ds(2 * N + j * TILE, TILE)
        own = slice(j * TILE, (j + 1) * TILE)
        x = conv(nn(normed_ref[...], w1_s[:, FRONT + j * TILE : FRONT + (j + 1) * TILE]), cols)
        x_ref[:, own] = x
        xf = x.astype(F32)
        hot = one_hot(j)
        dtx_ref[:, own] = (xf * wide(dt_parts, hot)).astype(BF16)
        pay_ref[:N, own] = nn(b_turned, (xf * wide(both_parts, hot)).astype(BF16)).astype(BF16)
        extra = [nn(p, hot)[:1] for p in through_parts]
        pay_ref[N:, own] = jnp.concatenate(extra + [jnp.zeros((HALO - 3, TILE), F32)], axis=0).astype(BF16)
    for copy in written:
        copy.wait()


def first_stage(tok, gain_in, meta, taps, hp, p, q, total):
    (po, px, masks_p, lin_p), (qo, qx, masks_q, _) = p, q
    ext = total + HALO
    return pl.pallas_call(
        functools.partial(first_kernel, masks_p, masks_q, total),
        out_shape=(
            shape((D, W1_COLS), BF16), shape((ext, D), BF16), shape((ext, CONV), BF16), shape((total, CONV), BF16), shape((total, 2 * N), BF16),
            shape((total, INNER), BF16), shape((total, INNER), BF16), shape((5, total, N)), shape((H, total)), shape((N + HALO, INNER), BF16),
        ),
        in_specs=[SMEM] + [VMEM] * 8 + [ANY] * 4,
        out_specs=(HBM, VMEM, HBM, HBM) + tuple([VMEM] * 6),
        scratch_shapes=[pltpu.VMEM((ext, TILE), F32), pltpu.VMEM((D, W1_COLS), BF16), pltpu.VMEM((ext, CONV), BF16), pltpu.VMEM((total, CONV), BF16), pltpu.SemaphoreType.DMA((len(masks_p),)), pltpu.SemaphoreType.DMA((len(masks_q),)), pltpu.SemaphoreType.DMA((2 * (INNER // TILE + 1) + 1,))],
        compiler_params=params(),
        cost_estimate=SMALL,
        name="first_stage",
    )(lin_p, *tok, gain_in, meta, taps, hp, po, px, qo, qx)


def late_copies(count, blocks, wg_s, wo_s, sem_g, sem_o):
    rows = D // count
    first, second = [], []
    for r in range(count):
        copy = pltpu.make_async_copy(blocks.at[r, 0], wg_s.at[pl.ds(r * rows, rows)], sem_g.at[r])
        copy.start()
        first.append(copy)
    for r in range(count):
        for i in range(2):
            target = wo_s.at[pl.ds((2 * r + i) * rows, rows)]
            copy = pltpu.make_async_copy(blocks.at[r, 1, :, pl.ds(i * D, D)], target, sem_o.at[2 * r + i])
            copy.start()
            second.append(copy)
    return first, second


def late_scratch(count):
    return [pltpu.VMEM((D, INNER), BF16), pltpu.VMEM((INNER, D), BF16), pltpu.SemaphoreType.DMA((count,)), pltpu.SemaphoreType.DMA((2 * count,))]


def gate_kernel(count, normed_ref, g_ref, blocks, ga_ref, dga_ref, gno_ref, wg_s, wo_s, sem_g, sem_o):
    first, second = late_copies(count, blocks, wg_s, wo_s, sem_g, sem_o)
    for copy in first:
        copy.wait()
    for j in range(INNER // TILE):
        own = slice(j * TILE, (j + 1) * TILE)
        gate = nn(normed_ref[HALO:], wg_s[:, own])
        sig = sigmoid(gate)
        ga_ref[:, own] = (gate * sig).astype(BF16)
        dga_ref[:, own] = (sig * (1.0 + gate * (1.0 - sig))).astype(BF16)
    for copy in second:
        copy.wait()
    for j in range(INNER // TILE):
        own = slice(j * TILE, (j + 1) * TILE)
        gno_ref[:, own] = nt(g_ref[...], wo_s[own, :]).astype(BF16)


def gate_stage(normed, g, blocks, total):
    count = blocks.shape[0]
    return pl.pallas_call(
        functools.partial(gate_kernel, count),
        out_shape=(shape((total, INNER), BF16),) * 3,
        in_specs=[VMEM] * 2 + [HBM],
        out_specs=tuple([VMEM] * 3),
        scratch_shapes=late_scratch(count),
        compiler_params=params(),
        cost_estimate=SMALL,
        name="gate_stage",
    )(normed, g, blocks)


def left_lanes():
    return lax.broadcasted_iota(jnp.int32, (1, 2 * P_SIZE), 1) < P_SIZE


def pairs_kernel(total, bc_ref, dtx_ref, cumt_ref, id_col, id_row, out_ref, cb_ref, mask_ref):
    @pl.when(pl.program_id(0) == 0)
    def _():
        cb_ref[...] = nt(bc_ref[:, N:], bc_ref[:, :N])
        row = lax.broadcasted_iota(jnp.int32, (total, total), 0)
        col = lax.broadcasted_iota(jnp.int32, (total, total), 1)
        mask_ref[...] = jnp.where((row >= col) & (id_col[...] == id_row[...]), 0.0, -1e30)

    cum_cols = cumt_ref[...].T
    left = left_lanes()
    for pair in range(GROUP // 2):
        lanes = slice(pair * 2 * P_SIZE, (pair + 1) * 2 * P_SIZE)
        for a in range(total // N):
            rows, width = slice(a * N, (a + 1) * N), (a + 1) * N
            made = []
            for i in (2 * pair, 2 * pair + 1):
                decay = jnp.exp(cum_cols[rows, i : i + 1] - cumt_ref[i : i + 1, :width] + mask_ref[rows, :width])
                made.append(nn((decay * cb_ref[rows, :width]).astype(BF16), dtx_ref[:width, lanes]))
            out_ref[rows, lanes] = jnp.where(left, made[0], made[1])


def pairs_stage(bc, dtx, cumt, id_col, id_row, total):
    block = pl.BlockSpec((total, GROUP * P_SIZE), lambda g: (0, g))
    return pl.pallas_call(
        functools.partial(pairs_kernel, total),
        grid=(H // GROUP,),
        out_shape=shape((total, INNER)),
        in_specs=[VMEM, block, pl.BlockSpec((GROUP, total), lambda g: (g, 0)), VMEM, VMEM],
        out_specs=block,
        scratch_shapes=[pltpu.VMEM((total, total), F32)] * 2,
        compiler_params=params(),
        cost_estimate=SMALL,
        name="pairs_stage",
    )(bc, dtx, cumt, id_col, id_row)


def pairs_back_kernel(total, bc_ref, dtx_ref, e_ref, cumt_ref, id_col, id_row, gdtx_ref, gb_ref, gc_ref, cb_ref, mask_ref, acc_ref):
    @pl.when(pl.program_id(0) == 0)
    def _():
        cb_ref[...] = nt(bc_ref[:, :N], bc_ref[:, N:])
        row = lax.broadcasted_iota(jnp.int32, (total, total), 0)
        col = lax.broadcasted_iota(jnp.int32, (total, total), 1)
        mask_ref[...] = jnp.where((row <= col) & (id_col[...] == id_row[...]), 0.0, -1e30)
        acc_ref[...] = jnp.zeros_like(acc_ref)

    cum_cols = cumt_ref[...].T
    left = left_lanes()
    for pair in range(GROUP // 2):
        lanes = slice(pair * 2 * P_SIZE, (pair + 1) * 2 * P_SIZE)
        for a in range(total // N):
            rows, after = slice(a * N, (a + 1) * N), slice(a * N, total)
            made, added = [], None
            for side, i in enumerate((2 * pair, 2 * pair + 1)):
                decay = jnp.exp(cumt_ref[i : i + 1, after] - cum_cols[rows, i : i + 1] + mask_ref[rows, after])
                made.append(nn((decay * cb_ref[rows, after]).astype(BF16), e_ref[after, lanes]))
                mine = dtx_ref[rows, lanes].astype(F32)
                mine = jnp.where(left, mine, 0.0) if side == 0 else jnp.where(left, 0.0, mine)
                term = nt(mine.astype(BF16), e_ref[after, lanes]) * decay
                added = term if added is None else added + term
            gdtx_ref[rows, lanes] = jnp.where(left, made[0], made[1])
            acc_ref[rows, after] += added

    @pl.when(pl.program_id(0) == H // GROUP - 1)
    def _():
        gb_ref[...] = nn(acc_ref[...].astype(BF16), bc_ref[:, N:])
        gc_ref[...] = nn(acc_ref[...].T.astype(BF16), bc_ref[:, :N])


def pairs_back_stage(bc, dtx, e, cumt, id_col, id_row, total):
    block = pl.BlockSpec((total, GROUP * P_SIZE), lambda g: (0, g))
    flat = pl.BlockSpec((total, N), lambda g: (0, 0))
    return pl.pallas_call(
        functools.partial(pairs_back_kernel, total),
        grid=(H // GROUP,),
        out_shape=(shape((total, INNER)), shape((total, N)), shape((total, N))),
        in_specs=[VMEM, block, block, pl.BlockSpec((GROUP, total), lambda g: (g, 0)), VMEM, VMEM],
        out_specs=(block, flat, flat),
        scratch_shapes=[pltpu.VMEM((total, total), F32)] * 3,
        compiler_params=params(),
        cost_estimate=SMALL,
        name="pairs_back_stage",
    )(bc, dtx, e, cumt, id_col, id_row)


def combined(refs, cols):
    states = refs[0][:N, cols].astype(F32)
    factor = None
    for near, ref in zip(refs, refs[1:]):
        step = jnp.sum(near[N:, cols].astype(F32), axis=0, keepdims=True)
        factor = step if factor is None else factor * step
        states = states + factor * ref[:N, cols].astype(F32)
    return states


def output_kernel(count, total, *refs):
    got = refs[:count]
    (inside_ref, bc_ref, x_ref, hd_ref, ga_ref, dga_ref, gno_ref, gain_ref, skip_ref, own_ref,
     state_ref, no_ref, e_ref, gg_ref, pay_ref, gc_ref, rows_ref, ggain_ref, scan_s, gated_s) = refs[count:]
    c_part = bc_ref[:, N:]
    reach = packed(hd_ref[2])
    squares = jnp.zeros((total, 1), F32)
    crossed = jnp.zeros((total, 1), F32)
    for j in range(INNER // TILE):
        own = slice(j * TILE, (j + 1) * TILE)
        state = combined(got, own).astype(BF16)
        state_ref[:, own] = state
        scan = inside_ref[:, own] + nn(c_part, state) * wide(reach, one_hot(j))
        scan_s[:, own] = scan
        mixed = (scan + skip_ref[:, own] * x_ref[:, own].astype(F32)).astype(BF16)
        gg_ref[:, own] = mixed
        gated = mixed.astype(F32) * ga_ref[:, own].astype(F32)
        gated_s[:, own] = gated
        squares = squares + jnp.sum(gated * gated, axis=-1, keepdims=True)
        crossed = crossed + jnp.sum(gno_ref[:, own].astype(F32) * gain_ref[:, own] * gated, axis=-1, keepdims=True)
    scale = lax.rsqrt(squares / INNER + EPS)
    mean = crossed * scale / INNER
    c_turned = turned(c_part).astype(BF16)
    grad_c = jnp.zeros((total, N), F32)
    row_sum = jnp.zeros((total, N), F32)
    for j in range(INNER // TILE):
        own = slice(j * TILE, (j + 1) * TILE)
        hot = one_hot(j)
        unit = gated_s[:, own] * scale
        gno = gno_ref[:, own].astype(F32)
        no_ref[:, own] = (unit * gain_ref[:, own]).astype(BF16)
        ggain_ref[:, own] = jnp.sum(gno * unit, axis=0, keepdims=True)
        grad = scale * (gno * gain_ref[:, own] - unit * mean)
        e = (grad * ga_ref[:, own].astype(F32)).astype(BF16)
        e_ref[:, own] = e
        gg_ref[:, own] = (grad * gg_ref[:, own].astype(F32) * dga_ref[:, own].astype(F32)).astype(BF16)
        ef = e.astype(F32)
        e_reach = (ef * wide(reach, hot)).astype(BF16)
        pay_ref[:N, own] = nn(c_turned, e_reach).astype(BF16)
        grad_c = grad_c + nt(e_reach, state_ref[:, own])
        row_sum = row_sum + head_sum(ef * scan_s[:, own], hot)
    pay_ref[N:, :] = own_ref[N:, :]
    gc_ref[...] = grad_c
    rows_ref[...] = row_sum


def output_stage(got, inside, bc, x, hd, ga, dga, gno, gain_out, skip_wide, pay, total):
    count = len(got)
    big = lambda t: shape((total, INNER), t)
    return pl.pallas_call(
        functools.partial(output_kernel, count, total),
        out_shape=(shape((N, INNER), BF16), big(BF16), big(BF16), big(BF16), shape((N + HALO, INNER), BF16), shape((total, N)), shape((total, N)), shape((1, INNER))),
        in_specs=[VMEM] * (count + 10),
        out_specs=tuple([VMEM] * 8),
        scratch_shapes=[pltpu.VMEM((total, INNER), F32)] * 2,
        compiler_params=params(),
        cost_estimate=SMALL,
        name="output_stage",
    )(*got, inside, bc, x, hd, ga, dga, gno, gain_out, skip_wide, pay)


def turn_kernel(count, tab_p, tab_q, normed_ref, p_ref, q_ref):
    rows = D // count
    for j in range(D // TILE):
        made = normed_ref[:, j * TILE : (j + 1) * TILE].astype(F32).T.astype(BF16)
        for i in range(TILE // rows):
            block = made[i * rows : (i + 1) * rows]
            a = j * (TILE // rows) + i
            p_ref[pl.ds(pl.multiple_of(tab_p[a] * rows, rows), rows), :] = block
            q_ref[pl.ds(pl.multiple_of(tab_q[a] * rows, rows), rows), :] = block


def turn_stage(tab_p, tab_q, normed):
    out = shape((D, normed.shape[0]), BF16)
    return pl.pallas_call(
        functools.partial(turn_kernel, tab_p.shape[0]),
        out_shape=(out, out),
        in_specs=[SMEM, SMEM, VMEM],
        out_specs=(VMEM, VMEM),
        compiler_params=params(),
        cost_estimate=SMALL,
        name="turn_stage",
    )(tab_p, tab_q, normed)


def weights_kernel(count, tab_q, turned_ref, gg_ref, no_ref, g_ref, keep_g, send_g, keep_o, send_o, turned_s):
    for j in range(INNER // TILE):
        own = slice(j * TILE, (j + 1) * TILE)
        weight_grad(turned_ref[:, HALO:], gg_ref[:, own], own, keep_g, send_g)
    rows = INNER // count
    for j in range(INNER // TILE):
        made = no_ref[:, j * TILE : (j + 1) * TILE].astype(F32).T.astype(BF16)
        for i in range(TILE // rows):
            place = pl.ds(pl.multiple_of(tab_q[j * (TILE // rows) + i] * rows, rows), rows)
            turned_s[place, :] = made[i * rows : (i + 1) * rows]
    for j in range(D // TILE):
        own = slice(j * TILE, (j + 1) * TILE)
        weight_grad(turned_s[...], g_ref[:, own], own, keep_o, send_o)


def weights_stage(tab_q, turned_rows, grad_gate, normed_out, g, total):
    return pl.pallas_call(
        functools.partial(weights_kernel, tab_q.shape[0]),
        out_shape=(shape((D // 2, INNER), BF16),) * 2 + (shape((D, D), BF16),) * 2,
        in_specs=[SMEM] + [VMEM] * 4,
        out_specs=tuple([VMEM] * 4),
        scratch_shapes=[pltpu.VMEM((INNER, total), BF16)],
        compiler_params=params(),
        cost_estimate=SMALL,
        name="weights_stage",
    )(tab_q, turned_rows, grad_gate, normed_out, g)


def rest_kernel(count, no_ref, gg_ref, tok_ref, blocks, out_ref, part_ref, wg_s, wo_s, sem_g, sem_o):
    first, second = late_copies(count, blocks, wg_s, wo_s, sem_g, sem_o)
    for copy in first:
        copy.wait()
    half = D // 4
    for j in range(4):
        own = slice(j * half, (j + 1) * half)
        part_ref[:, own] = nt(gg_ref[...], wg_s[own, :])
    for copy in second:
        copy.wait()
    for j in range(4):
        own = slice(j * half, (j + 1) * half)
        out_ref[:, own] = (tok_ref[HALO:, own].astype(F32) + nn(no_ref[...], wo_s[:, own])).astype(BF16)


def rest_stage(normed_out, grad_gate, ext_tok, blocks, total):
    count = blocks.shape[0]
    return pl.pallas_call(
        functools.partial(rest_kernel, count),
        out_shape=(shape((total, D), BF16), shape((total, D))),
        in_specs=[VMEM] * 3 + [HBM],
        out_specs=(VMEM, VMEM),
        scratch_shapes=late_scratch(count),
        compiler_params=params(),
        cost_estimate=SMALL,
        name="rest_stage",
    )(normed_out, grad_gate, ext_tok, blocks)


def heads_back(count, total, tiles, got, refs, sums, emit):
    gdtx_ref, e_ref, x_ref, dtx_ref, bc_ref, state_ref, hd_ref, skip_ref = refs
    gb, q_sum, back_sum, xg, both, gskip = sums
    b_part = bc_ref[:, :N]
    dt_parts, end_parts = packed(hd_ref[0]), packed(hd_ref[3])
    for n, j in enumerate(tiles):
        own = slice(j * TILE, (j + 1) * TILE)
        hot = one_hot(j)
        later = combined(got, own)
        later_low = later.astype(BF16)
        w_end, dt = wide(end_parts, hot), wide(dt_parts, hot)
        from_later = nn(b_part, later_low) * w_end
        inner = gdtx_ref[:, own]
        dtx = dtx_ref[:, own].astype(F32)
        x, e = x_ref[:, own].astype(F32), e_ref[:, own].astype(F32)
        q_sum = q_sum + head_sum(dtx * from_later, hot)
        back_sum = back_sum + head_sum(dtx * inner, hot)
        grad = inner + from_later
        xg = xg + head_sum(x * grad, hot)
        crossing = jnp.sum(state_ref[:, own].astype(F32) * later, axis=0, keepdims=True)
        skipped = jnp.sum(x * e, axis=0, keepdims=True)
        both = both + head_sum(jnp.broadcast_to(crossing, (8, TILE)), hot)
        gskip = gskip + head_sum(jnp.broadcast_to(skipped, (8, TILE)), hot)
        gb = gb + nt((dtx * w_end).astype(BF16), later_low)
        emit(n, j, (dt * grad + skip_ref[:, own] * e).astype(BF16).astype(F32))
    return gb, q_sum, back_sum, xg, both, gskip


def conv_back(total, grad_act, cols, place, conv_refs, ext_s, cin_s):
    pre_ref, cin_ref, taps_ref, meta_ref, gt_ref = conv_refs
    pre = pre_ref[:, cols].astype(F32)
    sig = sigmoid(pre)
    cin_s[...] = cin_ref[:, cols].astype(F32)
    grad = grad_act * sig * (1.0 + pre * (1.0 - sig))
    gt_ref[KERNEL : KERNEL + 1, place] = jnp.sum(grad, axis=0, keepdims=True)
    ext_s[...] = jnp.zeros_like(ext_s)
    for k in range(KERNEL):
        masked = grad if k == 3 else grad * meta_ref[:, k : k + 1]
        rows = slice(HALO - 3 + k, HALO - 3 + k + total)
        gt_ref[k : k + 1, place] = jnp.sum(masked * cin_s[rows, :], axis=0, keepdims=True)
        ext_s[rows, :] += masked * taps_ref[k : k + 1, cols]
    return ext_s[...].astype(BF16)


def weight_grad(turned, grads, place, keep_ref, send_ref):
    made = nn(turned, grads)
    half = made.shape[0] // 2
    keep_ref[:, place] = made[:half].astype(BF16)
    send_ref[:, place] = made[half:].astype(BF16)


def back_kernel(count, total, last, small, *refs):
    got, refs = refs[:count], refs[count:]
    heads, refs = refs[:8], refs[8:]
    pre_ref, cin_ref, taps_ref, meta_ref, turned_ref = refs[:5]
    refs = refs[5:]
    if last:
        acc_in, few_in, gcs_ref, gcp_ref, gbp_ref, rows_ref, hp_ref = refs[:7]
        refs = refs[7:]
        if small:
            gt_first, gout_ref, tab = refs[:3]
            refs = refs[3:]
    keep_ref, send_ref, proj_ref, gt_ref, acc_ref, few_ref, ext_s, cin_s = refs[:8]
    conv_refs = (pre_ref, cin_ref, taps_ref, meta_ref, gt_ref)
    gt_ref[...] = jnp.zeros_like(gt_ref)
    base = FRONT if last else 0

    def emit(n, j, grad_x):
        place = slice(base + n * TILE, base + (n + 1) * TILE)
        grads = conv_back(total, grad_x, slice(2 * N + j * TILE, 2 * N + (j + 1) * TILE), place, conv_refs, ext_s, cin_s)
        proj_ref[:, place] = grads
        weight_grad(turned_ref[...], grads, place, keep_ref, send_ref)

    tiles = range(P_TILES) if last else range(P_TILES, INNER // TILE)
    if last:
        sums = tuple(acc_in[i] for i in range(4)) + (few_in[0], few_in[1])
    else:
        zero = jnp.zeros((total, N), F32)
        sums = (zero,) * 4 + (jnp.zeros((8, N), F32),) * 2
    gb, q_sum, back_sum, xg, both, gskip = heads_back(count, total, tiles, got, heads, sums, emit)
    if not last:
        acc_ref[0], acc_ref[1], acc_ref[2], acc_ref[3] = gb, q_sum, back_sum, xg
        few_ref[0], few_ref[1] = both, gskip
        return
    hd_ref = heads[6]
    grad_bc = jnp.concatenate([gb + gbp_ref[...], gcs_ref[...] + gcp_ref[...]], axis=1)
    place = slice(128, FRONT)
    proj_ref[:, place] = conv_back(total, grad_bc, slice(0, 2 * N), place, conv_refs, ext_s, cin_s)
    row = lax.broadcasted_iota(jnp.int32, (total, total), 0)
    col = lax.broadcasted_iota(jnp.int32, (total, total), 1)
    upper = (row <= col).astype(F32).astype(BF16)
    below = (row > col).astype(F32).astype(BF16)
    dt, reach, shifted, rate = hd_ref[0], hd_ref[2], hd_ref[4], hp_ref[1:2, :]
    grad_ld = exact_sum(upper, rows_ref[...] - back_sum) + exact_sum(below, q_sum) + both[0:1] * reach[total - 1 : total]
    grad_step = (xg - grad_ld * rate) * meta_ref[:, 3:4] * sigmoid(shifted)
    grad_step = jnp.where(lax.broadcasted_iota(jnp.int32, grad_step.shape, 1) < H, grad_step, 0.0)
    proj_ref[:HALO, :128] = jnp.zeros((HALO, 128), BF16)
    proj_ref[HALO:, :128] = grad_step.astype(BF16)
    few_ref[0] = jnp.broadcast_to(jnp.sum(grad_step, axis=0, keepdims=True), (8, N))
    few_ref[1] = jnp.broadcast_to(jnp.sum(grad_ld * (-dt * rate), axis=0, keepdims=True), (8, N))
    few_ref[2] = gskip
    acc_ref[...] = jnp.zeros_like(acc_ref)
    if not small:
        weight_grad(turned_ref[...], proj_ref[:, :FRONT], slice(0, FRONT), keep_ref, send_ref)
        return
    small_s, front_s, conv_s = refs[8:]
    grad_small(*small, tab, gt_ref, gt_first, gout_ref, few_ref, small_s, conv_s)
    made = nn(turned_ref[...], proj_ref[:, :FRONT])
    front_s[...] = made[:, :128]
    rows = D // small[0]
    for r in range(small[0]):
        front_s[r * rows : r * rows + 8, :] += pltpu.roll(small_s[r], H, 1)
    half = D // 2
    keep_ref[:, :128], send_ref[:, :128] = front_s[:half].astype(BF16), front_s[half:].astype(BF16)
    keep_ref[:, 128:FRONT], send_ref[:, 128:FRONT] = made[:half, 128:].astype(BF16), made[half:, 128:].astype(BF16)


def back_stage(got, heads, conv_refs, turned_rows, more, total, small=()):
    last = bool(more)
    width = P_COLS if last else Q_COLS
    ext = total + HALO
    acc = shape((1, 8, N)) if last else shape((4, total, N))
    scratch = [pltpu.VMEM((ext, TILE), F32)] * 2
    if small:
        scratch += [pltpu.VMEM((small[0], 8, 128), F32), pltpu.VMEM((D, 128), F32), pltpu.VMEM((8, CONV), F32)]
    return pl.pallas_call(
        functools.partial(back_kernel, len(got), total, last, small),
        out_shape=(shape((D // 2, width), BF16), shape((D // 2, width), BF16), shape((ext, width), BF16), shape((8, width)), acc, shape((3 if last else 2, 8, N))),
        in_specs=[VMEM] * (len(got) + 13 + len(more) - bool(small)) + [SMEM] * bool(small),
        out_specs=tuple([VMEM] * 6),
        scratch_shapes=scratch,
        compiler_params=params(),
        cost_estimate=SMALL,
        name="back_last" if last else "back_first",
    )(*got, *heads, *conv_refs, turned_rows, *more)


def normed_kernel(pp_ref, pq_ref, w1_ref, part_ref, out_ref):
    out_ref[...] = nt(pp_ref[:, 128:], w1_ref[:, 128:P_COLS]) + nt(pq_ref[...], w1_ref[:, P_COLS:])
    out_ref[...] += nt(pp_ref[:, :H], w1_ref[:, :H])
    out_ref[HALO:, :] += part_ref[...]


def normed_stage(proj_p, proj_q, w1, part):
    return pl.pallas_call(
        normed_kernel,
        out_shape=shape((proj_p.shape[0], D)),
        in_specs=[VMEM] * 4,
        out_specs=VMEM,
        compiler_params=params(),
        cost_estimate=SMALL,
        name="normed_stage",
    )(proj_p, proj_q, w1, part)


def body(tokens, scene_ids, valid_mask, norm_gain, w_in, conv_w, conv_b, dt_bias, a_log, d_skip, gate_gain, w_out, d_out):
    n_f, n_s = lax.axis_size("fsdp"), lax.axis_size("seq")
    n_dev = n_f * n_s
    s_rank = lax.axis_index("seq")
    lin = lax.axis_index("fsdp") * n_s + s_rank
    rows = tokens.shape[2]
    total, length = MB * rows, n_s * rows
    r_in, r_out = w_in.shape[0], w_out.shape[0]
    f_bits = [n_s << b for b in range(n_f.bit_length() - 1)]
    s_bits = [1 << b for b in range(n_s.bit_length() - 1)]
    n_x = len(f_bits) - 1
    z, x, y = combos(s_bits[n_x:]), combos(s_bits[:n_x]), combos(f_bits[1:])
    xy, core = combos(s_bits[:n_x] + f_bits[1:]), [n_s]
    orders = [order_of([z, x, y, core]), order_of([z, y, x, core]), order_of([z, xy, core])]
    aligned = r_in % 16 == 0
    tables = jnp.asarray(np.stack([np.argsort(o) for o in orders]), jnp.int32)[:, jnp.arange(n_dev) ^ lin]

    inverse3 = pow(3, -1, n_s)
    source = lambda i: [((3 * d + i) % n_s, d) for d in range(n_s)]

    def chosen(arr, i):
        d = (inverse3 * (s_rank - i + n_s)) % n_s
        return lax.select_n((3 * d + i + MB * n_s) // n_s % MB, arr[0, 0], arr[1, 0], arr[2, 0])

    def home(parts):
        return [lax.ppermute(part, "seq", [(d, k) for k, d in source(i)]) for i, part in enumerate(parts)]

    def placed(blocks):
        return jnp.stack([lax.select_n((m * n_s + s_rank) % MB, *blocks) for m in range(MB)])[:, None]

    late = jnp.concatenate([w_in[:, :INNER], jnp.concatenate([w_out[: r_out // 2], w_out[r_out // 2 :]], axis=1)])
    spare = 128 - H
    line = lambda v: jnp.pad(v.astype(F32), ((0, 0), (0, (spare if aligned else 128) - v.shape[1])))
    heads = jnp.concatenate([dt_bias, a_log, d_skip])[None]
    small = jnp.concatenate([line(conv_w), line(conv_b[None]), line(norm_gain[None]), line(gate_gain[None]), line(heads)])
    if aligned:
        pad = jnp.pad(jnp.concatenate(split3(small)), ((0, r_in - 24), (0, 0)))
    else:
        pad = jnp.zeros((r_in, spare), BF16)
    w1 = jnp.concatenate([w_in[:, INNER + CONV :], pad, w_in[:, 2 * INNER : INNER + CONV], w_in[:, INNER : 2 * INNER]], axis=1)

    first = spread(w1[None], z)
    halo = lax.ppermute(chosen(tokens, -1)[rows - HALO :], "seq", source(-1))
    first, halo, tokens, d_out, tables, late = tied(first, halo, tokens, d_out, tables, late)
    tab_small = tables[2]
    tab_p, tab_q = (tables[0], tables[1]) if aligned else (jnp.arange(32, dtype=jnp.int32),) * 2
    p, q = first[..., :P_COLS], first[..., P_COLS:]
    got = [lax.ppermute(chosen(tokens, i), "seq", source(i)) for i in range(MB)]
    picked = [chosen(d_out, i) for i in range(MB)]
    p, q, picked, *got = tied(spread(p, x), spread(q, y), picked, *got)
    g = [lax.ppermute(picked[i], "seq", source(i)) for i in range(MB)]
    ids = (scene_ids[:, 0] + 8 * jnp.arange(MB, dtype=jnp.int32)[:, None]).reshape(1, -1)
    lines = jnp.concatenate([jnp.pad(ids, ((0, 0), (HALO, 0)), constant_values=-1), jnp.pad(valid_mask[:, 0].reshape(1, -1), ((0, 0), (HALO, 0)))])
    lines = lax.dynamic_slice_in_dim(lines, s_rank * total, total + HALO, axis=1)
    lines = jnp.pad(lines.astype(F32), ((0, 6), (0, -(total + HALO) % 128)))
    p, q, lines, *g = tied(spread(p, y), spread(q, x), lines, *g)
    p_other, q_other = permute(p, n_s), permute(q, n_s)
    if aligned:
        small = jnp.concatenate([p[:, :, :128], p_other[:, :, :128]])
        tab_small = tab_p
    else:
        small = jnp.pad(small, ((0, 8 - small.shape[0]), (0, 0)))[None]
        for stage in (z, xy, core):
            small = spread(small, stage)
    taps, gain_in, gain_out, hp, skip_wide, meta, id_col, id_row = small_stage(tab_small, small, lines, n_dev, n_s, total)

    late = lax.all_gather(late, BOTH, axis=0, tiled=True).reshape(n_dev, 2, r_in, INNER)
    if not aligned:
        wg = late[:, 0].reshape(32, D // 32, INNER)
        wo = late[:, 1].reshape(n_dev, r_in, 2, D).transpose(0, 2, 1, 3).reshape(32, 2, D // 32, D)
        late = jnp.stack([wg, wo.transpose(0, 2, 1, 3).reshape(32, D // 32, INNER)], axis=1)

    def pieces(own, other, which):
        if aligned:
            return own, other, orders[which], lin[None]
        both = jnp.concatenate([own, other])[tables[which]]
        both = both.reshape(32, D // 32, both.shape[2])
        return both[:16], both[16:], np.arange(32), jnp.zeros((1,), jnp.int32)

    w1_full, normed, conv_in, conv_pre, bc, x_part, dtx, hd, cumt, pay = first_stage(
        (halo, *got), gain_in, meta, taps, hp, pieces(p, p_other, 0), pieces(q, q_other, 1), total
    )

    def spans(k):
        return [d for d in range(n_s - k) if ((d + 1) * total - 1) // length == (d + k) * total // length]

    far = max(k for k in range(1, n_s) if spans(k))
    pay, normed, dtx, cumt = tied(pay, normed, dtx, cumt)
    before = [lax.ppermute(pay, "seq", [(d, d + k) for d in spans(k)]) for k in range(1, far + 1)]
    normed_p, normed_q = turn_stage(tab_p, tab_q, normed)
    inside = pairs_stage(bc, dtx, cumt, id_col, id_row, total)
    g = jnp.concatenate(g)
    ga, dga, gno = gate_stage(normed, g, late, total)
    inside, normed_p, normed_q, gno, *before = tied(inside, normed_p, normed_q, gno, *before)
    state_in, normed_out, e, grad_gate, pay_back, gc_state, row_sum, grad_gain_out = output_stage(
        before, inside, bc, x_part, hd, ga, dga, gno, gain_out, skip_wide, pay, total
    )

    adjoints = [None if k == 2 else lax.ppermute(pay_back, "seq", [(d + k, d) for d in spans(k)]) for k in range(1, far + 1)]

    def sent(keep, send, which):
        if aligned:
            return keep, send
        both = jnp.concatenate([keep, send])
        both = both.reshape(n_dev, -1, both.shape[1])[jnp.asarray(orders[which]) ^ lin].reshape(both.shape)
        return both[: keep.shape[0]], both[keep.shape[0] :]

    ext_tok = jnp.concatenate([halo] + got)
    blocks = lambda v: v.reshape(n_dev // 2, -1, v.shape[1])
    keep_g, send_g, keep_o, send_o = weights_stage(tab_q, normed_p, grad_gate, normed_out, g, total)
    gdtx, gb_pairs, gc_pairs = pairs_back_stage(bc, dtx, e, cumt, id_col, id_row, total)
    rg, ro = sent(keep_g, send_g, 0), sent(keep_o, send_o, 1)
    (rg, ro), gdtx, gb_pairs, gc_pairs, normed_out, pay_back, near, *more = tied(
        (rg, ro), gdtx, gb_pairs, gc_pairs, normed_out, pay_back, adjoints[0], *adjoints[2:]
    )
    adjoints = [near] + [lax.ppermute(pay_back, "seq", [(d + 2, d) for d in spans(2)])] + more
    block_out, part = rest_stage(normed_out, grad_gate, ext_tok, late, total)
    rg, ro = cut(blocks(fold(rg, core)), y), cut(blocks(fold(ro, core)), x)
    (rg, ro), gdtx, block_out, part, *adjoints = tied((rg, ro), gdtx, block_out, part, *adjoints)

    conv_refs = (conv_pre, conv_in, taps, meta)
    head_refs = (gdtx, e, x_part, dtx, bc, state_in, hd, skip_wide)
    keep_q, send_q, proj_q, gt_q, acc, few = back_stage(adjoints, head_refs, conv_refs, normed_q, (), total)
    rg, ro = cut(fold(rg, y), x), cut(fold(ro, x), y)
    thirds = lambda v: [v[i * rows : (i + 1) * rows] for i in range(MB)]
    block_out = home(thirds(block_out))
    rq = sent(keep_q, send_q, 1)
    (rg, ro, rq), proj_q, gt_q, acc, few, block_out = tied((rg, ro, rq), proj_q, gt_q, acc, few, block_out)

    more = (acc, few, gc_state, gc_pairs, gb_pairs, row_sum, hp) + ((gt_q, grad_gain_out, tab_p) if aligned else ())
    keep_p, send_p, proj_p, gt_p, _, few = back_stage(
        adjoints, head_refs, conv_refs, normed_p, more, total, (n_dev, n_s) if aligned else ()
    )
    rg, ro = fold(rg, x), fold(ro, y)
    ro = jnp.concatenate([ro[:, : r_out // 2], ro[:, r_out // 2 :]], axis=2)
    both = cut(jnp.stack([rg, ro], axis=1), z)
    rp = sent(keep_p, send_p, 0)
    (both, rq, rp), proj_p, gt_p, few, block_out = tied((both, rq, rp), proj_p, gt_p, few, block_out)

    grad_normed = normed_stage(proj_p, proj_q, w1_full, part)
    both = fold(both, z, F32)[0]
    rp, rq = cut(blocks(fold(rp, core)), y), cut(blocks(fold(rq, core)), x)
    (rp, rq), both, grad_normed = tied((rp, rq), both, grad_normed)
    rim = lax.ppermute(grad_normed[:HALO], "seq", [(d + 1, d) for d in range(n_s - 1)])
    rp, rq = cut(fold(rp, y), x), cut(fold(rq, x), y)
    (rp, rq), rim, grad_normed = tied((rp, rq), rim, grad_normed)
    own = grad_normed[HALO:]
    own = jnp.concatenate([own[: total - HALO], own[total - HALO :] + rim])
    u = ext_tok[HALO:].astype(F32)
    in_scale = lax.rsqrt(jnp.mean(u * u, axis=-1, keepdims=True) + EPS)
    unit, q_in = u * in_scale, own * gain_in
    grad_in = (g.astype(F32) + in_scale * (q_in - unit * jnp.mean(q_in * unit, axis=-1, keepdims=True))).astype(BF16)
    grad_in = home(thirds(grad_in))
    w1_grad = cut(jnp.concatenate([fold(rp, x), fold(rq, y)], axis=2), z)
    w1_grad, grad_in, block_out = tied(w1_grad, grad_in, block_out)
    w1_grad = fold(w1_grad, z, F32)[0]
    if aligned:
        small = w1_grad[:8, H:128]
    else:
        small = grad_small_stage(tab_small, gt_p, gt_q, grad_gain_out, few, n_dev, n_s)
        for stage in (core, xy, z):
            small = fold(cut(small, stage), stage, F32)
        small = small[0]
    block_out, grad_in = placed(block_out), placed(grad_in)
    out_wo = jnp.concatenate([both[1, :, :D], both[1, :, D:]], axis=0)
    out_win = jnp.concatenate([both[0], w1_grad[:, FRONT:], w1_grad[:, 128:FRONT], w1_grad[:, :H]], axis=1)
    grad_gain = jnp.sum(out_win * w_in.astype(F32), axis=1) / norm_gain.astype(F32)
    count = dt_bias.shape[0]
    head = lambda k: small[7, k * count : (k + 1) * count]
    return (
        block_out, grad_in, grad_gain, out_win, small[:KERNEL, : conv_b.shape[0]], small[KERNEL, : conv_b.shape[0]],
        head(0), head(1), head(2), small[6, :r_out], out_wo,
    )


def solution(mesh):
    tok = P(None, "fsdp", "seq", None)
    row = P(None, "fsdp", None)
    specs = (tok, row, row, P(BOTH), P(BOTH, None), P(None, BOTH), P(BOTH), P("seq"), P("seq"), P("seq"), P(BOTH), P(BOTH, None), tok)
    outs = (tok, tok, P(BOTH), P(BOTH, None), P(None, BOTH), P(BOTH), P("seq"), P("seq"), P("seq"), P(BOTH), P(BOTH, None))
    return jax.shard_map(body, mesh=mesh, in_specs=specs, out_specs=outs, check_vma=False)
```

```python
import functools

import numpy as np
import jax
import jax.numpy as jnp
from jax import lax
from jax.experimental import pallas as pl
from jax.experimental.pallas import tpu as pltpu
from jax.sharding import PartitionSpec as P

D = 1024
H = 32
P_SIZE = 64
N = 128
KERNEL = 4
MB = 3
INNER = H * P_SIZE
CONV = INNER + 2 * N
HALO = 16
FRONT = 384
TILE = 256
P_TILES = 3
P_COLS = FRONT + P_TILES * TILE
W1_COLS = FRONT + INNER
Q_COLS = W1_COLS - P_COLS
GROUP = 8
EPS = 1e-05
F32 = jnp.float32
BF16 = jnp.bfloat16
BOTH = ("fsdp", "seq")
VMEM = pl.BlockSpec(memory_space=pltpu.VMEM)
SMEM = pl.BlockSpec(memory_space=pltpu.SMEM)
ANY = pl.BlockSpec(memory_space=pl.ANY)
HBM = pl.BlockSpec(memory_space=pltpu.HBM)
SMALL = pl.CostEstimate(flops=1, bytes_accessed=1, transcendentals=0)


def shape(dims, dtype=F32):
    return jax.ShapeDtypeStruct(dims, dtype)


def params(mib=27):
    return pltpu.CompilerParams(vmem_limit_bytes=mib * 2**20)


def permute(block, mask):
    size = lax.axis_size("fsdp") * lax.axis_size("seq")
    return lax.ppermute(block, BOTH, [(i, i ^ mask) for i in range(size)])


def tied(*values):
    return lax.optimization_barrier(values)


def combos(masks):
    found = [0]
    for mask in masks:
        found += [c | mask for c in found]
    return found[1:]


def spread(held, stage):
    return jnp.concatenate([held] + [permute(held, m) for m in stage], axis=0)


def cut(total, stage):
    width = total.shape[0] // (len(stage) + 1)
    return [total[i * width : (i + 1) * width] for i in range(len(stage) + 1)]


def fold(pieces, stage, dtype=BF16):
    total = pieces[0].astype(F32)
    for part, m in zip(pieces[1:], stage):
        total = total + permute(part, m).astype(F32)
    return total.astype(dtype)


def fold_cut(pieces, stage, after):
    parts = [permute(part, m) for part, m in zip(pieces[1:], stage)]
    made = []
    for cuts in zip(*[cut(v, after) for v in [pieces[0]] + parts]):
        total = cuts[0].astype(F32)
        for part in cuts[1:]:
            total = total + part.astype(F32)
        made.append(total.astype(BF16))
    return made


def order_of(stages):
    masks = [0]
    for stage in stages:
        held = list(masks)
        for m in stage:
            masks += [k ^ m for k in held]
    return np.array(masks, np.int32)


def split3(v):
    high = lax.reduce_precision(v, 8, 7)
    mid = lax.reduce_precision(v - high, 8, 7)
    return [p.astype(BF16) for p in (high, mid, v - high - mid)]


def nn(a, b):
    return jnp.dot(a, b, preferred_element_type=F32)


def nt(a, b):
    return lax.dot_general(a, b, (((1,), (1,)), ((), ())), preferred_element_type=F32)


def tn(a, b):
    return lax.dot_general(a, b, (((0,), (0,)), ((), ())), preferred_element_type=F32)


def split(v, count=3):
    parts = []
    for _ in range(count):
        part = v.astype(BF16)
        parts.append(part)
        v = v - part.astype(F32)
    return parts


def one_hot(tile):
    row = lax.broadcasted_iota(jnp.int32, (N, TILE), 0)
    col = lax.broadcasted_iota(jnp.int32, (N, TILE), 1)
    return ((row % H == tile * (TILE // P_SIZE) + col // P_SIZE) & (row < 3 * H)).astype(F32).astype(BF16)


def packed(v):
    lane = lax.broadcasted_iota(jnp.int32, v.shape, 1)
    v = jnp.where(lane < H, v, 0.0)
    high, mid, low = [p.astype(F32) for p in split(v)]
    return (high + pltpu.roll(mid, H, 1) + pltpu.roll(low, 2 * H, 1)).astype(BF16)


def wide(parts, hot):
    return nn(parts, hot)


def head_sum(v, hot):
    return sum(nt(p, hot) for p in split(v, 2))


def sigmoid(v):
    return 1.0 / (1.0 + jnp.exp(-v))


def exact_sum(matrix, v):
    return sum(nn(matrix, p) for p in split(v))


def turned(v):
    return v.astype(F32).T


def block_copies(lin, masks, sources, place, sems):
    copies = []
    half = len(masks) // 2
    for r, mask in enumerate(masks):
        where = lin ^ int(mask)
        source = sources[r // half].at[r % half]
        for src, dst in place(source, where):
            copy = pltpu.make_async_copy(src, dst, sems.at[len(copies)])
            copy.start()
            copies.append(copy)
    return copies


def rows_at(ref, where, height, cols):
    return ref.at[pl.ds(pl.multiple_of(where * height, height), height), cols]


def put(out_ref, piece, offset, width, rows):
    first, shift = offset // 128, offset % 128
    lane = lax.broadcasted_iota(jnp.int32, piece.shape, 1)
    moved = pltpu.roll(jnp.where(lane < width, piece, 0.0), shift, 1) if shift else jnp.where(lane < width, piece, 0.0)
    if shift + width > 128:
        out_ref[rows, first * 128 : first * 128 + 128] += jnp.where(lane >= shift, moved, 0.0)
        out_ref[rows, first * 128 + 128 : first * 128 + 256] += jnp.where(lane < shift, moved, 0.0)
    else:
        out_ref[rows, first * 128 : first * 128 + 128] += moved


def get(in_ref, offset, width, rows):
    first, shift = offset // 128, offset % 128
    piece = in_ref[rows, first * 128 : first * 128 + 128]
    lane = lax.broadcasted_iota(jnp.int32, piece.shape, 1)
    if shift + width > 128:
        piece = jnp.where(lane >= shift, piece, in_ref[rows, first * 128 + 128 : first * 128 + 256])
    piece = pltpu.roll(piece, 128 - shift, 1) if shift else piece
    return jnp.where(lane < width, piece, 0.0)


def small_kernel(n_dev, n_s, total, part, tab, small_ref, line_ref, taps_ref, gin_ref, gout_ref, hp_ref, skip_ref, meta_ref, col_ref, row_ref, conv_s):
    conv_s[...] = jnp.zeros_like(conv_s)
    gin_ref[...] = jnp.zeros_like(gin_ref)
    gout_ref[...] = jnp.zeros_like(gout_ref)
    hp_ref[...] = jnp.zeros_like(hp_ref)
    channels, features, wider, heads = CONV // n_dev, D // n_dev, INNER // n_dev, H // n_s
    everything = slice(0, 8)
    for d in range(n_dev):
        block = small_ref[tab[d]]
        if part:
            block = block.astype(F32)
            block = pltpu.roll(block[:8] + block[8:16] + block[16:24], 128 - H, 1)
        put(conv_s, block, d * channels, channels, everything)
        put(gin_ref, block[5:6], d * features, features, slice(0, 1))
        put(gout_ref, block[6:7], d * wider, wider, slice(0, 1))
        if d < n_s:
            for k in range(3):
                head = block[7:8] if k == 0 else pltpu.roll(block[7:8], 128 - k * heads, 1)
                put(hp_ref, head, d * heads, heads, slice(k, k + 1))
    taps_ref[:, : 2 * N] = conv_s[:, INNER:]
    taps_ref[:, 2 * N :] = conv_s[:, :INNER]
    lane = lax.broadcasted_iota(jnp.int32, (1, N), 1)
    hp_ref[1:2, :] = jnp.where(lane < H, jnp.exp(hp_ref[1:2, :]), 0.0)
    parts = packed(jnp.broadcast_to(hp_ref[2:3, :], (16, N)))
    for j in range(INNER // TILE):
        skip_ref[:, j * TILE : (j + 1) * TILE] = wide(parts, one_hot(j))[:1]
    line = line_ref[...]
    wide_line = line.shape[1]
    moved = lambda v, k: pltpu.roll(v, wide_line - k, 1)[:, :total]
    ids = line[0:1]
    own = moved(ids, HALO)
    keep = lambda test: jnp.where(test, 1.0, 0.0)
    same = [keep(moved(ids, HALO - 3 + k) == own) for k in range(3)]
    before = jnp.sum(jnp.where(lax.broadcasted_iota(jnp.int32, ids.shape, 1) == HALO - 1, ids, 0.0), axis=1, keepdims=True)
    final = jnp.sum(jnp.where(lax.broadcasted_iota(jnp.int32, ids.shape, 1) == HALO + total - 1, ids, 0.0), axis=1, keepdims=True)
    rows = same + [moved(line[1:2], HALO), keep(own == before), keep(own == final), own, own]
    turned_rows = jnp.concatenate(rows, axis=0).T
    meta_ref[...] = turned_rows
    col_ref[...] = turned_rows[:, 6:7]
    row_ref[...] = own


def small_stage(tab, small, line, n_dev, n_s, total):
    return pl.pallas_call(
        functools.partial(small_kernel, n_dev, n_s, total, small.dtype == BF16),
        out_shape=(
            shape((8, CONV)), shape((1, D)), shape((1, INNER)), shape((8, N)), shape((1, INNER)), shape((total, 8)), shape((total, 1)), shape((1, total)),
        ),
        in_specs=[SMEM, VMEM, VMEM],
        out_specs=tuple([VMEM] * 8),
        scratch_shapes=[pltpu.VMEM((8, CONV), F32)],
        compiler_params=params(),
        cost_estimate=SMALL,
        name="small_stage",
    )(tab, small, line)


def grad_small(n_dev, n_s, tab, gp_ref, gq_ref, gout_ref, few_ref, out_ref, conv_s):
    split_at = P_TILES * TILE
    conv_s[:, :split_at] = gp_ref[:, FRONT:]
    conv_s[:, split_at:INNER] = gq_ref[...]
    conv_s[:, INNER:] = gp_ref[:, 128:FRONT]
    channels, wider, heads = CONV // n_dev, INNER // n_dev, H // n_s
    for d in range(n_dev):
        where = (d % n_s) * heads
        head = jnp.zeros((1, 128), F32)
        for k in range(3):
            piece = get(few_ref.at[k], where, heads, slice(0, 1))
            head = head + (pltpu.roll(piece, k * heads, 1) if k else piece)
        rows = [get(conv_s, d * channels, channels, slice(0, 8))[:5], jnp.zeros((1, 128), F32)]
        rows += [get(gout_ref, d * wider, wider, slice(0, 1)), head]
        out_ref[tab[d]] = jnp.concatenate(rows, axis=0)


def grad_small_stage(tab, gp, gq, gout, few, n_dev, n_s):
    return pl.pallas_call(
        functools.partial(grad_small, n_dev, n_s),
        out_shape=shape((n_dev, 8, 128)),
        in_specs=[SMEM] + [VMEM] * 4,
        out_specs=VMEM,
        scratch_shapes=[pltpu.VMEM((8, CONV), F32)],
        compiler_params=params(),
        cost_estimate=SMALL,
        name="grad_small_stage",
    )(tab, gp, gq, gout, few)


def weight_copies(lin, masks_p, masks_q, po, px, qo, qx, w1_s, sem_p, sem_q):
    rows = D // len(masks_p)
    place = lambda cols: lambda src, where: [(src, rows_at(w1_s, where, rows, cols))]
    first = block_copies(lin, masks_p, (po, px), place(pl.ds(0, P_COLS)), sem_p)
    second = block_copies(lin, masks_q, (qo, qx), place(pl.ds(P_COLS, Q_COLS)), sem_q)
    return first, second


def first_kernel(masks_p, masks_q, total, lin_ref, halo_ref, t0_ref, t1_ref, t2_ref, gain_ref, meta_ref, taps_ref, hp_ref, po, px, qo, qx,
                 normed_ref, cin_ref, pre_ref, bc_ref, x_ref, dtx_ref, hd_ref, cumt_ref, pay_ref, cin_s, w1_s, cin_b, pre_b, sem_p, sem_q, sem_out):
    first, second = weight_copies(lin_ref[0], masks_p, masks_q, po, px, qo, qx, w1_s, sem_p, sem_q)
    start = 0
    for ref in (halo_ref, t0_ref, t1_ref, t2_ref):
        u = ref[...].astype(F32)
        scale = lax.rsqrt(jnp.mean(u * u, axis=-1, keepdims=True) + EPS)
        normed_ref[start : start + u.shape[0], :] = (u * scale * gain_ref[...]).astype(BF16)
        start += u.shape[0]
    written = []

    def write(source, target):
        copy = pltpu.make_async_copy(source, target, sem_out.at[len(written)])
        copy.start()
        written.append(copy)

    for copy in first:
        copy.wait()
    meta = meta_ref[...]
    same = [meta[:, k : k + 1] for k in range(3)]
    valid, carry, tail = meta[:, 3:4], meta[:, 4:5], meta[:, 5:6]

    def conv(made, cols):
        cin_s[...] = made
        cin_b[:, cols] = made.astype(BF16)
        acc = taps_ref[4:5, cols] + taps_ref[3:4, cols] * made[HALO:]
        for k in range(3):
            acc = acc + taps_ref[k : k + 1, cols] * (cin_s[HALO - 3 + k : HALO - 3 + k + total, :] * same[k])
        pre_b[:, cols] = acc.astype(BF16)
        write(cin_b.at[:, cols], cin_ref.at[:, cols])
        write(pre_b.at[:, cols], pre_ref.at[:, cols])
        return (acc * sigmoid(acc)).astype(BF16)

    front = nn(normed_ref[...], w1_s[:, :FRONT])
    lane = lax.broadcasted_iota(jnp.int32, (total, 128), 1)
    shifted = jnp.where(lane < H, front[HALO:, :128], 0.0).astype(BF16).astype(F32) + hp_ref[0:1, :]
    dt = (jnp.maximum(shifted, 0.0) + jnp.log1p(jnp.exp(-jnp.abs(shifted)))) * valid
    row = lax.broadcasted_iota(jnp.int32, (total, total), 0)
    col = lax.broadcasted_iota(jnp.int32, (total, total), 1)
    lower = (row >= col).astype(F32).astype(BF16)
    cum = exact_sum(lower, -dt * hp_ref[1:2, :])
    reach = jnp.exp(cum) * carry
    w_end = jnp.exp(cum[total - 1 : total] - cum) * tail
    hd_ref[0], hd_ref[1], hd_ref[2], hd_ref[3], hd_ref[4] = dt, cum, reach, w_end, shifted
    cumt_ref[...] = cum.T[:H]
    bc = conv(front[:, 128:], pl.ds(0, 2 * N))
    bc_ref[...] = bc
    b_turned = turned(bc[:, :N]).astype(BF16)
    through = jnp.broadcast_to(reach[total - 1 : total], (8, N))
    dt_parts, both_parts = packed(dt), packed(dt * w_end)
    through_parts = [packed(p.astype(F32)) for p in split(through)]
    for j in range(INNER // TILE):
        if j == P_TILES:
            for copy in second:
                copy.wait()
        cols = pl.ds(2 * N + j * TILE, TILE)
        own = slice(j * TILE, (j + 1) * TILE)
        x = conv(nn(normed_ref[...], w1_s[:, FRONT + j * TILE : FRONT + (j + 1) * TILE]), cols)
        x_ref[:, own] = x
        xf = x.astype(F32)
        hot = one_hot(j)
        dtx_ref[:, own] = (xf * wide(dt_parts, hot)).astype(BF16)
        pay_ref[:N, own] = nn(b_turned, (xf * wide(both_parts, hot)).astype(BF16)).astype(BF16)
        extra = [nn(p, hot)[:1] for p in through_parts]
        pay_ref[N:, own] = jnp.concatenate(extra + [jnp.zeros((HALO - 3, TILE), F32)], axis=0).astype(BF16)
    for copy in written:
        copy.wait()


def first_stage(tok, gain_in, meta, taps, hp, p, q, total):
    (po, px, masks_p, lin_p), (qo, qx, masks_q, _) = p, q
    ext = total + HALO
    return pl.pallas_call(
        functools.partial(first_kernel, masks_p, masks_q, total),
        out_shape=(
            shape((ext, D), BF16), shape((ext, CONV), BF16), shape((total, CONV), BF16), shape((total, 2 * N), BF16),
            shape((total, INNER), BF16), shape((total, INNER), BF16), shape((5, total, N)), shape((H, total)), shape((N + HALO, INNER), BF16),
        ),
        in_specs=[SMEM] + [VMEM] * 8 + [ANY] * 4,
        out_specs=(VMEM, HBM, HBM) + tuple([VMEM] * 6),
        scratch_shapes=[pltpu.VMEM((ext, TILE), F32), pltpu.VMEM((D, W1_COLS), BF16), pltpu.VMEM((ext, CONV), BF16), pltpu.VMEM((total, CONV), BF16), pltpu.SemaphoreType.DMA((len(masks_p),)), pltpu.SemaphoreType.DMA((len(masks_q),)), pltpu.SemaphoreType.DMA((2 * (INNER // TILE + 1),))],
        compiler_params=params(),
        cost_estimate=SMALL,
        name="first_stage",
    )(lin_p, *tok, gain_in, meta, taps, hp, po, px, qo, qx)


def late_copies(count, blocks, wg_s, wo_s, sem_g, sem_o):
    rows = D // count
    first, second = [], []
    for r in range(count):
        copy = pltpu.make_async_copy(blocks.at[r, 0], wg_s.at[pl.ds(r * rows, rows)], sem_g.at[r])
        copy.start()
        first.append(copy)
    for r in range(count):
        for i in range(2):
            target = wo_s.at[pl.ds((2 * r + i) * rows, rows)]
            copy = pltpu.make_async_copy(blocks.at[r, 1, :, pl.ds(i * D, D)], target, sem_o.at[2 * r + i])
            copy.start()
            second.append(copy)
    return first, second


def late_scratch(count):
    return [pltpu.VMEM((D, INNER), BF16), pltpu.VMEM((INNER, D), BF16), pltpu.SemaphoreType.DMA((count,)), pltpu.SemaphoreType.DMA((2 * count,))]


def gate_kernel(count, normed_ref, g_ref, blocks, ga_ref, dga_ref, gno_ref, wg_s, wo_s, sem_g, sem_o):
    first, second = late_copies(count, blocks, wg_s, wo_s, sem_g, sem_o)
    for copy in first:
        copy.wait()
    for j in range(INNER // TILE):
        own = slice(j * TILE, (j + 1) * TILE)
        gate = nn(normed_ref[HALO:], wg_s[:, own])
        sig = sigmoid(gate)
        ga_ref[:, own] = (gate * sig).astype(BF16)
        dga_ref[:, own] = (sig * (1.0 + gate * (1.0 - sig))).astype(BF16)
    for copy in second:
        copy.wait()
    for j in range(INNER // TILE):
        own = slice(j * TILE, (j + 1) * TILE)
        gno_ref[:, own] = nt(g_ref[...], wo_s[own, :]).astype(BF16)


def gate_stage(normed, g, blocks, total):
    count = blocks.shape[0]
    return pl.pallas_call(
        functools.partial(gate_kernel, count),
        out_shape=(shape((total, INNER), BF16),) * 3,
        in_specs=[VMEM] * 2 + [HBM],
        out_specs=tuple([VMEM] * 3),
        scratch_shapes=late_scratch(count),
        compiler_params=params(40),
        cost_estimate=SMALL,
        name="gate_stage",
    )(normed, g, blocks)


def left_lanes():
    return lax.broadcasted_iota(jnp.int32, (1, 2 * P_SIZE), 1) < P_SIZE


def pairs_kernel(total, bc_ref, dtx_ref, cumt_ref, id_col, id_row, out_ref, cb_ref, mask_ref):
    @pl.when(pl.program_id(0) == 0)
    def _():
        cb_ref[...] = nt(bc_ref[:, N:], bc_ref[:, :N])
        row = lax.broadcasted_iota(jnp.int32, (total, total), 0)
        col = lax.broadcasted_iota(jnp.int32, (total, total), 1)
        mask_ref[...] = jnp.where((row >= col) & (id_col[...] == id_row[...]), 0.0, -1e30)

    cum_cols = cumt_ref[...].T
    left = left_lanes()
    for pair in range(GROUP // 2):
        lanes = slice(pair * 2 * P_SIZE, (pair + 1) * 2 * P_SIZE)
        for a in range(total // N):
            rows, width = slice(a * N, (a + 1) * N), (a + 1) * N
            made = []
            for i in (2 * pair, 2 * pair + 1):
                decay = jnp.exp(cum_cols[rows, i : i + 1] - cumt_ref[i : i + 1, :width] + mask_ref[rows, :width])
                made.append(nn((decay * cb_ref[rows, :width]).astype(BF16), dtx_ref[:width, lanes]))
            out_ref[rows, lanes] = jnp.where(left, made[0], made[1])


def pairs_stage(bc, dtx, cumt, id_col, id_row, total):
    block = pl.BlockSpec((total, GROUP * P_SIZE), lambda g: (0, g))
    return pl.pallas_call(
        functools.partial(pairs_kernel, total),
        grid=(H // GROUP,),
        out_shape=shape((total, INNER)),
        in_specs=[VMEM, block, pl.BlockSpec((GROUP, total), lambda g: (g, 0)), VMEM, VMEM],
        out_specs=block,
        scratch_shapes=[pltpu.VMEM((total, total), F32)] * 2,
        compiler_params=params(),
        cost_estimate=SMALL,
        name="pairs_stage",
    )(bc, dtx, cumt, id_col, id_row)


def pairs_back_kernel(total, bc_ref, dtx_ref, e_ref, cumt_ref, id_col, id_row, gdtx_ref, gb_ref, gc_ref, cb_ref, mask_ref, acc_ref):
    @pl.when(pl.program_id(0) == 0)
    def _():
        cb_ref[...] = nt(bc_ref[:, :N], bc_ref[:, N:])
        row = lax.broadcasted_iota(jnp.int32, (total, total), 0)
        col = lax.broadcasted_iota(jnp.int32, (total, total), 1)
        mask_ref[...] = jnp.where((row <= col) & (id_col[...] == id_row[...]), 0.0, -1e30)
        acc_ref[...] = jnp.zeros_like(acc_ref)

    cum_cols = cumt_ref[...].T
    left = left_lanes()
    for pair in range(GROUP // 2):
        lanes = slice(pair * 2 * P_SIZE, (pair + 1) * 2 * P_SIZE)
        for a in range(total // N):
            rows, after = slice(a * N, (a + 1) * N), slice(a * N, total)
            made, added = [], None
            for side, i in enumerate((2 * pair, 2 * pair + 1)):
                decay = jnp.exp(cumt_ref[i : i + 1, after] - cum_cols[rows, i : i + 1] + mask_ref[rows, after])
                made.append(nn((decay * cb_ref[rows, after]).astype(BF16), e_ref[after, lanes]))
                mine = dtx_ref[rows, lanes].astype(F32)
                mine = jnp.where(left, mine, 0.0) if side == 0 else jnp.where(left, 0.0, mine)
                term = nt(mine.astype(BF16), e_ref[after, lanes]) * decay
                added = term if added is None else added + term
            gdtx_ref[rows, lanes] = jnp.where(left, made[0], made[1])
            acc_ref[rows, after] += added

    @pl.when(pl.program_id(0) == H // GROUP - 1)
    def _():
        gb_ref[...] = nn(acc_ref[...].astype(BF16), bc_ref[:, N:])
        gc_ref[...] = nn(acc_ref[...].T.astype(BF16), bc_ref[:, :N])


def pairs_back_stage(bc, dtx, e, cumt, id_col, id_row, total):
    block = pl.BlockSpec((total, GROUP * P_SIZE), lambda g: (0, g))
    flat = pl.BlockSpec((total, N), lambda g: (0, 0))
    return pl.pallas_call(
        functools.partial(pairs_back_kernel, total),
        grid=(H // GROUP,),
        out_shape=(shape((total, INNER)), shape((total, N)), shape((total, N))),
        in_specs=[VMEM, block, block, pl.BlockSpec((GROUP, total), lambda g: (g, 0)), VMEM, VMEM],
        out_specs=(block, flat, flat),
        scratch_shapes=[pltpu.VMEM((total, total), F32)] * 3,
        compiler_params=params(),
        cost_estimate=SMALL,
        name="pairs_back_stage",
    )(bc, dtx, e, cumt, id_col, id_row)


def combined(refs, cols):
    states = refs[0][:N, cols].astype(F32)
    factor = None
    for near, ref in zip(refs, refs[1:]):
        step = jnp.sum(near[N:, cols].astype(F32), axis=0, keepdims=True)
        factor = step if factor is None else factor * step
        states = states + factor * ref[:N, cols].astype(F32)
    return states


def double_kernel(own_ref, next_ref, out_ref):
    for j in range(INNER // TILE):
        cols = slice(j * TILE, (j + 1) * TILE)
        factor = jnp.sum(own_ref[N:, cols].astype(F32), axis=0, keepdims=True)
        further = jnp.sum(next_ref[N:, cols].astype(F32), axis=0, keepdims=True)
        out_ref[:N, cols] = (own_ref[:N, cols].astype(F32) + factor * next_ref[:N, cols].astype(F32)).astype(BF16)
        parts = [p.astype(F32) for p in split(factor * further)]
        out_ref[N:, cols] = jnp.concatenate(parts + [jnp.zeros((HALO - 3, TILE), F32)], axis=0).astype(BF16)


def double_stage(own, following):
    return pl.pallas_call(
        double_kernel,
        out_shape=shape(own.shape, BF16),
        in_specs=[VMEM] * 2,
        out_specs=VMEM,
        compiler_params=params(),
        cost_estimate=SMALL,
        name="double_stage",
    )(own, following)


def output_kernel(count, total, *refs):
    got = refs[:count]
    (inside_ref, bc_ref, x_ref, hd_ref, ga_ref, dga_ref, gno_ref, gain_ref, skip_ref, own_ref,
     state_ref, no_ref, e_ref, gg_ref, pay_ref, gc_ref, rows_ref, ggain_ref, scan_s, gated_s) = refs[count:]
    c_part = bc_ref[:, N:]
    reach = packed(hd_ref[2])
    squares = jnp.zeros((total, 1), F32)
    crossed = jnp.zeros((total, 1), F32)
    for j in range(INNER // TILE):
        own = slice(j * TILE, (j + 1) * TILE)
        state = combined(got, own).astype(BF16)
        state_ref[:, own] = state
        scan = inside_ref[:, own] + nn(c_part, state) * wide(reach, one_hot(j))
        scan_s[:, own] = scan
        mixed = (scan + skip_ref[:, own] * x_ref[:, own].astype(F32)).astype(BF16)
        gg_ref[:, own] = mixed
        gated = mixed.astype(F32) * ga_ref[:, own].astype(F32)
        gated_s[:, own] = gated
        squares = squares + jnp.sum(gated * gated, axis=-1, keepdims=True)
        crossed = crossed + jnp.sum(gno_ref[:, own].astype(F32) * gain_ref[:, own] * gated, axis=-1, keepdims=True)
    scale = lax.rsqrt(squares / INNER + EPS)
    mean = crossed * scale / INNER
    c_turned = turned(c_part).astype(BF16)
    grad_c = jnp.zeros((total, N), F32)
    row_sum = jnp.zeros((total, N), F32)
    for j in range(INNER // TILE):
        own = slice(j * TILE, (j + 1) * TILE)
        hot = one_hot(j)
        unit = gated_s[:, own] * scale
        gno = gno_ref[:, own].astype(F32)
        no_ref[:, own] = (unit * gain_ref[:, own]).astype(BF16)
        ggain_ref[:, own] = jnp.sum(gno * unit, axis=0, keepdims=True)
        grad = scale * (gno * gain_ref[:, own] - unit * mean)
        e = (grad * ga_ref[:, own].astype(F32)).astype(BF16)
        e_ref[:, own] = e
        gg_ref[:, own] = (grad * gg_ref[:, own].astype(F32) * dga_ref[:, own].astype(F32)).astype(BF16)
        ef = e.astype(F32)
        e_reach = (ef * wide(reach, hot)).astype(BF16)
        pay_ref[:N, own] = nn(c_turned, e_reach).astype(BF16)
        grad_c = grad_c + nt(e_reach, state_ref[:, own])
        row_sum = row_sum + head_sum(ef * scan_s[:, own], hot)
    pay_ref[N:, :] = own_ref[N:, :]
    gc_ref[...] = grad_c
    rows_ref[...] = row_sum


def output_stage(got, inside, bc, x, hd, ga, dga, gno, gain_out, skip_wide, pay, total):
    count = len(got)
    big = lambda t: shape((total, INNER), t)
    return pl.pallas_call(
        functools.partial(output_kernel, count, total),
        out_shape=(shape((N, INNER), BF16), big(BF16), big(BF16), big(BF16), shape((N + HALO, INNER), BF16), shape((total, N)), shape((total, N)), shape((1, INNER))),
        in_specs=[VMEM] * (count + 10),
        out_specs=tuple([VMEM] * 8),
        scratch_shapes=[pltpu.VMEM((total, INNER), F32)] * 2,
        compiler_params=params(),
        cost_estimate=SMALL,
        name="output_stage",
    )(*got, inside, bc, x, hd, ga, dga, gno, gain_out, skip_wide, pay)


def turn_kernel(count, tab_p, tab_q, normed_ref, p_ref, q_ref):
    rows = D // count
    for j in range(D // TILE):
        made = normed_ref[:, j * TILE : (j + 1) * TILE].astype(F32).T.astype(BF16)
        for i in range(TILE // rows):
            block = made[i * rows : (i + 1) * rows]
            a = j * (TILE // rows) + i
            p_ref[pl.ds(pl.multiple_of(tab_p[a] * rows, rows), rows), :] = block
            q_ref[pl.ds(pl.multiple_of(tab_q[a] * rows, rows), rows), :] = block


def turn_stage(tab_p, tab_q, normed):
    out = shape((D, normed.shape[0]), BF16)
    return pl.pallas_call(
        functools.partial(turn_kernel, tab_p.shape[0]),
        out_shape=(out, out),
        in_specs=[SMEM, SMEM, VMEM],
        out_specs=(VMEM, VMEM),
        compiler_params=params(),
        cost_estimate=SMALL,
        name="turn_stage",
    )(tab_p, tab_q, normed)


def weights_kernel(count, tab_q, turned_ref, gg_ref, no_ref, g_ref, keep_g, send_g, keep_o, send_o, turned_s):
    for j in range(INNER // TILE):
        own = slice(j * TILE, (j + 1) * TILE)
        weight_grad(turned_ref[:, HALO:], gg_ref[:, own], own, keep_g, send_g)
    rows = INNER // count
    for j in range(INNER // TILE):
        made = no_ref[:, j * TILE : (j + 1) * TILE].astype(F32).T.astype(BF16)
        for i in range(TILE // rows):
            place = pl.ds(pl.multiple_of(tab_q[j * (TILE // rows) + i] * rows, rows), rows)
            turned_s[place, :] = made[i * rows : (i + 1) * rows]
    for j in range(D // TILE):
        own = slice(j * TILE, (j + 1) * TILE)
        weight_grad(turned_s[...], g_ref[:, own], own, keep_o, send_o)


def weights_stage(tab_q, turned_rows, grad_gate, normed_out, g, total):
    return pl.pallas_call(
        functools.partial(weights_kernel, tab_q.shape[0]),
        out_shape=(shape((D // 2, INNER), BF16),) * 2 + (shape((D, D), BF16),) * 2,
        in_specs=[SMEM] + [VMEM] * 4,
        out_specs=tuple([VMEM] * 4),
        scratch_shapes=[pltpu.VMEM((INNER, total), BF16)],
        compiler_params=params(),
        cost_estimate=SMALL,
        name="weights_stage",
    )(tab_q, turned_rows, grad_gate, normed_out, g)


def rest_kernel(count, no_ref, gg_ref, tok_ref, blocks, out_ref, part_ref, wg_s, wo_s, sem_g, sem_o):
    first, second = late_copies(count, blocks, wg_s, wo_s, sem_g, sem_o)
    for copy in first:
        copy.wait()
    half = D // 4
    for j in range(4):
        own = slice(j * half, (j + 1) * half)
        part_ref[:, own] = nt(gg_ref[...], wg_s[own, :])
    for copy in second:
        copy.wait()
    for j in range(4):
        own = slice(j * half, (j + 1) * half)
        out_ref[:, own] = (tok_ref[HALO:, own].astype(F32) + nn(no_ref[...], wo_s[:, own])).astype(BF16)


def rest_stage(normed_out, grad_gate, ext_tok, blocks, total):
    count = blocks.shape[0]
    return pl.pallas_call(
        functools.partial(rest_kernel, count),
        out_shape=(shape((total, D), BF16), shape((total, D))),
        in_specs=[VMEM] * 3 + [HBM],
        out_specs=(VMEM, VMEM),
        scratch_shapes=late_scratch(count),
        compiler_params=params(40),
        cost_estimate=SMALL,
        name="rest_stage",
    )(normed_out, grad_gate, ext_tok, blocks)


def heads_back(count, total, tiles, got, refs, sums, emit):
    gdtx_ref, e_ref, x_ref, dtx_ref, bc_ref, state_ref, hd_ref, skip_ref = refs
    gb, q_sum, back_sum, xg, both, gskip = sums
    b_part = bc_ref[:, :N]
    dt_parts, end_parts = packed(hd_ref[0]), packed(hd_ref[3])
    for n, j in enumerate(tiles):
        own = slice(j * TILE, (j + 1) * TILE)
        hot = one_hot(j)
        later = combined(got, own)
        later_low = later.astype(BF16)
        w_end, dt = wide(end_parts, hot), wide(dt_parts, hot)
        from_later = nn(b_part, later_low) * w_end
        inner = gdtx_ref[:, own]
        dtx = dtx_ref[:, own].astype(F32)
        x, e = x_ref[:, own].astype(F32), e_ref[:, own].astype(F32)
        q_sum = q_sum + head_sum(dtx * from_later, hot)
        back_sum = back_sum + head_sum(dtx * inner, hot)
        grad = inner + from_later
        xg = xg + head_sum(x * grad, hot)
        crossing = jnp.sum(state_ref[:, own].astype(F32) * later, axis=0, keepdims=True)
        skipped = jnp.sum(x * e, axis=0, keepdims=True)
        both = both + head_sum(jnp.broadcast_to(crossing, (8, TILE)), hot)
        gskip = gskip + head_sum(jnp.broadcast_to(skipped, (8, TILE)), hot)
        gb = gb + nt((dtx * w_end).astype(BF16), later_low)
        emit(n, j, (dt * grad + skip_ref[:, own] * e).astype(BF16).astype(F32))
    return gb, q_sum, back_sum, xg, both, gskip


def conv_back(total, grad_act, cols, place, conv_refs, ext_s, cin_s):
    pre_ref, cin_ref, taps_ref, meta_ref, gt_ref = conv_refs
    pre = pre_ref[:, cols].astype(F32)
    sig = sigmoid(pre)
    cin_s[...] = cin_ref[:, cols].astype(F32)
    grad = grad_act * sig * (1.0 + pre * (1.0 - sig))
    gt_ref[KERNEL : KERNEL + 1, place] = jnp.sum(grad, axis=0, keepdims=True)
    ext_s[...] = jnp.zeros_like(ext_s)
    for k in range(KERNEL):
        masked = grad if k == 3 else grad * meta_ref[:, k : k + 1]
        rows = slice(HALO - 3 + k, HALO - 3 + k + total)
        gt_ref[k : k + 1, place] = jnp.sum(masked * cin_s[rows, :], axis=0, keepdims=True)
        ext_s[rows, :] += masked * taps_ref[k : k + 1, cols]
    return ext_s[...].astype(BF16)


def weight_grad(turned, grads, place, keep_ref, send_ref):
    made = nn(turned, grads)
    half = made.shape[0] // 2
    keep_ref[:, place] = made[:half].astype(BF16)
    send_ref[:, place] = made[half:].astype(BF16)


def back_kernel(count, total, last, small, *refs):
    got, refs = refs[:count], refs[count:]
    heads, refs = refs[:8], refs[8:]
    pre_ref, cin_ref, taps_ref, meta_ref, turned_ref = refs[:5]
    refs = refs[5:]
    if last:
        acc_in, few_in, gcs_ref, gcp_ref, gbp_ref, rows_ref, hp_ref = refs[:7]
        refs = refs[7:]
        if small:
            gt_first, gout_ref, tab = refs[:3]
            refs = refs[3:]
    keep_ref, send_ref, proj_ref, gt_ref, acc_ref, few_ref, ext_s, cin_s = refs[:8]
    conv_refs = (pre_ref, cin_ref, taps_ref, meta_ref, gt_ref)
    gt_ref[...] = jnp.zeros_like(gt_ref)
    base = FRONT if last else 0

    def emit(n, j, grad_x):
        place = slice(base + n * TILE, base + (n + 1) * TILE)
        grads = conv_back(total, grad_x, slice(2 * N + j * TILE, 2 * N + (j + 1) * TILE), place, conv_refs, ext_s, cin_s)
        proj_ref[:, place] = grads
        weight_grad(turned_ref[...], grads, place, keep_ref, send_ref)

    tiles = range(P_TILES) if last else range(P_TILES, INNER // TILE)
    if last:
        sums = tuple(acc_in[i] for i in range(4)) + (few_in[0], few_in[1])
    else:
        zero = jnp.zeros((total, N), F32)
        sums = (zero,) * 4 + (jnp.zeros((8, N), F32),) * 2
    gb, q_sum, back_sum, xg, both, gskip = heads_back(count, total, tiles, got, heads, sums, emit)
    if not last:
        acc_ref[0], acc_ref[1], acc_ref[2], acc_ref[3] = gb, q_sum, back_sum, xg
        few_ref[0], few_ref[1] = both, gskip
        return
    hd_ref = heads[6]
    grad_bc = jnp.concatenate([gb + gbp_ref[...], gcs_ref[...] + gcp_ref[...]], axis=1)
    place = slice(128, FRONT)
    proj_ref[:, place] = conv_back(total, grad_bc, slice(0, 2 * N), place, conv_refs, ext_s, cin_s)
    row = lax.broadcasted_iota(jnp.int32, (total, total), 0)
    col = lax.broadcasted_iota(jnp.int32, (total, total), 1)
    upper = (row <= col).astype(F32).astype(BF16)
    below = (row > col).astype(F32).astype(BF16)
    dt, reach, shifted, rate = hd_ref[0], hd_ref[2], hd_ref[4], hp_ref[1:2, :]
    grad_ld = exact_sum(upper, rows_ref[...] - back_sum) + exact_sum(below, q_sum) + both[0:1] * reach[total - 1 : total]
    grad_step = (xg - grad_ld * rate) * meta_ref[:, 3:4] * sigmoid(shifted)
    grad_step = jnp.where(lax.broadcasted_iota(jnp.int32, grad_step.shape, 1) < H, grad_step, 0.0)
    proj_ref[:HALO, :128] = jnp.zeros((HALO, 128), BF16)
    proj_ref[HALO:, :128] = grad_step.astype(BF16)
    few_ref[0] = jnp.broadcast_to(jnp.sum(grad_step, axis=0, keepdims=True), (8, N))
    few_ref[1] = jnp.broadcast_to(jnp.sum(grad_ld * (-dt * rate), axis=0, keepdims=True), (8, N))
    few_ref[2] = gskip
    acc_ref[...] = jnp.zeros_like(acc_ref)
    if not small:
        weight_grad(turned_ref[...], proj_ref[:, :FRONT], slice(0, FRONT), keep_ref, send_ref)
        return
    small_s, front_s, conv_s = refs[8:]
    grad_small(*small, tab, gt_ref, gt_first, gout_ref, few_ref, small_s, conv_s)
    made = nn(turned_ref[...], proj_ref[:, :FRONT])
    front_s[...] = made[:, :128]
    rows = D // small[0]
    for r in range(small[0]):
        front_s[r * rows : r * rows + 8, :] += pltpu.roll(small_s[r], H, 1)
    half = D // 2
    keep_ref[:, :128], send_ref[:, :128] = front_s[:half].astype(BF16), front_s[half:].astype(BF16)
    keep_ref[:, 128:FRONT], send_ref[:, 128:FRONT] = made[:half, 128:].astype(BF16), made[half:, 128:].astype(BF16)


def back_stage(got, heads, conv_refs, turned_rows, more, total, small=()):
    last = bool(more)
    width = P_COLS if last else Q_COLS
    ext = total + HALO
    acc = shape((1, 8, N)) if last else shape((4, total, N))
    scratch = [pltpu.VMEM((ext, TILE), F32)] * 2
    if small:
        scratch += [pltpu.VMEM((small[0], 8, 128), F32), pltpu.VMEM((D, 128), F32), pltpu.VMEM((8, CONV), F32)]
    return pl.pallas_call(
        functools.partial(back_kernel, len(got), total, last, small),
        out_shape=(shape((D // 2, width), BF16), shape((D // 2, width), BF16), shape((ext, width), BF16), shape((8, width)), acc, shape((3 if last else 2, 8, N))),
        in_specs=[VMEM] * (len(got) + 13 + len(more) - bool(small)) + [SMEM] * bool(small),
        out_specs=tuple([VMEM] * 6),
        scratch_shapes=scratch,
        compiler_params=params(),
        cost_estimate=SMALL,
        name="back_last" if last else "back_first",
    )(*got, *heads, *conv_refs, turned_rows, *more)


def normed_kernel(masks_p, masks_q, lin_ref, pp_ref, pq_ref, part_ref, po, px, qo, qx, out_ref, w1_s, sem_p, sem_q):
    first, second = weight_copies(lin_ref[0], masks_p, masks_q, po, px, qo, qx, w1_s, sem_p, sem_q)
    for copy in first + second:
        copy.wait()
    out_ref[...] = nt(pp_ref[:, 128:], w1_s[:, 128:P_COLS]) + nt(pq_ref[...], w1_s[:, P_COLS:])
    out_ref[...] += nt(pp_ref[:, :H], w1_s[:, :H])
    out_ref[HALO:, :] += part_ref[...]


def normed_stage(proj_p, proj_q, part, p, q):
    (po, px, masks_p, lin), (qo, qx, masks_q, _) = p, q
    return pl.pallas_call(
        functools.partial(normed_kernel, masks_p, masks_q),
        out_shape=shape((proj_p.shape[0], D)),
        in_specs=[SMEM] + [VMEM] * 3 + [ANY] * 4,
        out_specs=VMEM,
        scratch_shapes=[pltpu.VMEM((D, W1_COLS), BF16), pltpu.SemaphoreType.DMA((len(masks_p),)), pltpu.SemaphoreType.DMA((len(masks_q),))],
        compiler_params=params(),
        cost_estimate=SMALL,
        name="normed_stage",
    )(lin, proj_p, proj_q, part, po, px, qo, qx)


def finish_kernel(normed_ref, rim_ref, tok_ref, g_ref, gain_ref, *outs):
    rows = outs[0].shape[0]
    for i, out_ref in enumerate(outs):
        own = slice(HALO + i * rows, HALO + (i + 1) * rows)
        u = tok_ref[own, :].astype(F32)
        scale = lax.rsqrt(jnp.mean(u * u, axis=-1, keepdims=True) + EPS)
        grad = normed_ref[own, :]
        if i == len(outs) - 1:
            grad = jnp.concatenate([grad[: rows - HALO], grad[rows - HALO :] + rim_ref[...]], axis=0)
        unit, q = u * scale, grad * gain_ref[...]
        out_ref[...] = (g_ref[i * rows : (i + 1) * rows, :].astype(F32) + scale * (q - unit * jnp.mean(q * unit, axis=-1, keepdims=True))).astype(BF16)


def finish_stage(grad_normed, rim, ext_tok, g, gain_in, rows):
    return pl.pallas_call(
        finish_kernel,
        out_shape=(shape((rows, D), BF16),) * MB,
        in_specs=[VMEM] * 5,
        out_specs=tuple([VMEM] * MB),
        compiler_params=params(),
        cost_estimate=SMALL,
        name="finish_stage",
    )(grad_normed, rim, ext_tok, g, gain_in)


def body(tokens, scene_ids, valid_mask, norm_gain, w_in, conv_w, conv_b, dt_bias, a_log, d_skip, gate_gain, w_out, d_out):
    n_f, n_s = lax.axis_size("fsdp"), lax.axis_size("seq")
    n_dev = n_f * n_s
    s_rank = lax.axis_index("seq")
    lin = lax.axis_index("fsdp") * n_s + s_rank
    rows = tokens.shape[2]
    total, length = MB * rows, n_s * rows
    r_in, r_out = w_in.shape[0], w_out.shape[0]
    f_bits = [n_s << b for b in range(n_f.bit_length() - 1)]
    s_bits = [1 << b for b in range(n_s.bit_length() - 1)]
    n_x = len(f_bits) - 1
    z, x, y = combos(s_bits[n_x:]), combos(s_bits[:n_x]), combos(f_bits[1:])
    xy, core = combos(s_bits[:n_x] + f_bits[1:]), [n_s]
    orders = [order_of([z, x, y, core]), order_of([z, y, x, core]), order_of([z, xy, core])]
    aligned = r_in % 16 == 0
    tables = jnp.asarray(np.stack([np.argsort(o) for o in orders]), jnp.int32)[:, jnp.arange(n_dev) ^ lin]

    inverse3 = pow(3, -1, n_s)
    source = lambda i: [((3 * d + i) % n_s, d) for d in range(n_s)]

    def chosen(arr, i):
        d = (inverse3 * (s_rank - i + n_s)) % n_s
        return lax.select_n((3 * d + i + MB * n_s) // n_s % MB, arr[0, 0], arr[1, 0], arr[2, 0])

    def home(parts):
        return [lax.ppermute(part, "seq", [(d, k) for k, d in source(i)]) for i, part in enumerate(parts)]

    def placed(blocks):
        return jnp.stack([lax.select_n((m * n_s + s_rank) % MB, *blocks) for m in range(MB)])[:, None]

    late = jnp.concatenate([w_in[:, :INNER], jnp.concatenate([w_out[: r_out // 2], w_out[r_out // 2 :]], axis=1)])
    spare = 128 - H
    line = lambda v: jnp.pad(v.astype(F32), ((0, 0), (0, (spare if aligned else 128) - v.shape[1])))
    heads = jnp.concatenate([dt_bias, a_log, d_skip])[None]
    small = jnp.concatenate([line(conv_w), line(conv_b[None]), line(norm_gain[None]), line(gate_gain[None]), line(heads)])
    if aligned:
        pad = jnp.pad(jnp.concatenate(split3(small)), ((0, r_in - 24), (0, 0)))
    else:
        pad = jnp.zeros((r_in, spare), BF16)
    w1 = jnp.concatenate([w_in[:, INNER + CONV :], pad, w_in[:, 2 * INNER : INNER + CONV], w_in[:, INNER : 2 * INNER]], axis=1)

    first = spread(w1[None], z)
    halo = lax.ppermute(chosen(tokens, -1)[rows - HALO :], "seq", source(-1))
    first, halo, tokens, d_out, tables, late = tied(first, halo, tokens, d_out, tables, late)
    tab_small = tables[2]
    tab_p, tab_q = (tables[0], tables[1]) if aligned else (jnp.arange(32, dtype=jnp.int32),) * 2
    p, q = first[..., :P_COLS], first[..., P_COLS:]
    got = [lax.ppermute(chosen(tokens, i), "seq", source(i)) for i in range(MB)]
    picked = [chosen(d_out, i) for i in range(MB)]
    p, q, picked, *got = tied(spread(p, x), spread(q, y), picked, *got)
    g = [lax.ppermute(picked[i], "seq", source(i)) for i in range(MB)]
    ids = (scene_ids[:, 0] + 8 * jnp.arange(MB, dtype=jnp.int32)[:, None]).reshape(1, -1)
    lines = jnp.concatenate([jnp.pad(ids, ((0, 0), (HALO, 0)), constant_values=-1), jnp.pad(valid_mask[:, 0].reshape(1, -1), ((0, 0), (HALO, 0)))])
    lines = lax.dynamic_slice_in_dim(lines, s_rank * total, total + HALO, axis=1)
    lines = jnp.pad(lines.astype(F32), ((0, 6), (0, -(total + HALO) % 128)))
    p, q, lines, *g = tied(spread(p, y), spread(q, x), lines, *g)
    p_other, q_other = permute(p, n_s), permute(q, n_s)
    if aligned:
        small = jnp.concatenate([p[:, :, :128], p_other[:, :, :128]])
        tab_small = tab_p
    else:
        small = jnp.pad(small, ((0, 8 - small.shape[0]), (0, 0)))[None]
        for stage in (z, xy, core):
            small = spread(small, stage)
    taps, gain_in, gain_out, hp, skip_wide, meta, id_col, id_row = small_stage(tab_small, small, lines, n_dev, n_s, total)

    late = lax.all_gather(late, BOTH, axis=0, tiled=True).reshape(n_dev, 2, r_in, INNER)
    if not aligned:
        wg = late[:, 0].reshape(32, D // 32, INNER)
        wo = late[:, 1].reshape(n_dev, r_in, 2, D).transpose(0, 2, 1, 3).reshape(32, 2, D // 32, D)
        late = jnp.stack([wg, wo.transpose(0, 2, 1, 3).reshape(32, D // 32, INNER)], axis=1)

    def pieces(own, other, which):
        if aligned:
            return own, other, orders[which], lin[None]
        both = jnp.concatenate([own, other])[tables[which]]
        both = both.reshape(32, D // 32, both.shape[2])
        return both[:16], both[16:], np.arange(32), jnp.zeros((1,), jnp.int32)

    piece_p, piece_q = pieces(p, p_other, 0), pieces(q, q_other, 1)
    normed, conv_in, conv_pre, bc, x_part, dtx, hd, cumt, pay = first_stage(
        (halo, *got), gain_in, meta, taps, hp, piece_p, piece_q, total
    )

    def spans(k):
        return [d for d in range(n_s - k) if ((d + 1) * total - 1) // length == (d + k) * total // length]

    far = max(k for k in range(1, n_s) if spans(k))
    reaches = [1 << b for b in range(far.bit_length())]
    pay, normed, dtx, cumt = tied(pay, normed, dtx, cumt)
    forth = lambda v, k: lax.ppermute(v, "seq", [(d, d + k) for d in spans(k)])
    before = [forth(pay, k) for k in range(1, far + 1)]
    normed_p, normed_q = turn_stage(tab_p, tab_q, normed)
    inside = pairs_stage(bc, dtx, cumt, id_col, id_row, total)
    g = jnp.concatenate(g)
    ga, dga, gno = gate_stage(normed, g, late, total)
    inside, normed_p, normed_q, gno, *before = tied(inside, normed_p, normed_q, gno, *before)
    state_in, normed_out, e, grad_gate, pay_back, gc_state, row_sum, grad_gain_out = output_stage(
        before, inside, bc, x_part, hd, ga, dga, gno, gain_out, skip_wide, pay, total
    )

    back = lambda v, k: lax.ppermute(v, "seq", [(d + k, d) for d in spans(k)])
    adjoints = [back(pay_back, 1)]

    def sent(keep, send, which):
        if aligned:
            return keep, send
        both = jnp.concatenate([keep, send])
        both = both.reshape(n_dev, -1, both.shape[1])[jnp.asarray(orders[which]) ^ lin].reshape(both.shape)
        return both[: keep.shape[0]], both[keep.shape[0] :]

    ext_tok = jnp.concatenate([halo] + got)
    blocks = lambda v: v.reshape(n_dev // 2, -1, v.shape[1])
    keep_g, send_g, keep_o, send_o = weights_stage(tab_q, normed_p, grad_gate, normed_out, g, total)
    gdtx, gb_pairs, gc_pairs = pairs_back_stage(bc, dtx, e, cumt, id_col, id_row, total)
    rg, ro = sent(keep_g, send_g, 0), sent(keep_o, send_o, 1)
    (rg, ro), gdtx, gb_pairs, gc_pairs, normed_out, pay_back, *adjoints = tied((rg, ro), gdtx, gb_pairs, gc_pairs, normed_out, pay_back, *adjoints)
    held = pay_back
    for k in reaches[1:]:
        held = double_stage(held, adjoints[-1])
        adjoints.append(back(held, k))
    block_out, part = rest_stage(normed_out, grad_gate, ext_tok, late, total)
    rg, ro = fold_cut([blocks(v) for v in rg], core, y), fold_cut([blocks(v) for v in ro], core, x)
    (rg, ro), gdtx, block_out, part, *adjoints = tied((rg, ro), gdtx, block_out, part, *adjoints)

    conv_refs = (conv_pre, conv_in, taps, meta)
    head_refs = (gdtx, e, x_part, dtx, bc, state_in, hd, skip_wide)
    keep_q, send_q, proj_q, gt_q, acc, few = back_stage(adjoints, head_refs, conv_refs, normed_q, (), total)
    rg, ro = fold_cut(rg, y, x), fold_cut(ro, x, y)
    thirds = lambda v: [v[i * rows : (i + 1) * rows] for i in range(MB)]
    block_out = home(thirds(block_out))
    rq = sent(keep_q, send_q, 1)
    (rg, ro, rq), proj_q, gt_q, acc, few, block_out = tied((rg, ro, rq), proj_q, gt_q, acc, few, block_out)

    more = (acc, few, gc_state, gc_pairs, gb_pairs, row_sum, hp) + ((gt_q, grad_gain_out, tab_p) if aligned else ())
    keep_p, send_p, proj_p, gt_p, _, few = back_stage(
        adjoints, head_refs, conv_refs, normed_p, more, total, (n_dev, n_s) if aligned else ()
    )
    rg, ro = fold(rg, x), fold(ro, y)
    ro = jnp.concatenate([ro[:, : r_out // 2], ro[:, r_out // 2 :]], axis=2)
    both = cut(jnp.stack([rg, ro], axis=1), z)
    rp = sent(keep_p, send_p, 0)
    (both, rq, rp), proj_p, gt_p, few, block_out = tied((both, rq, rp), proj_p, gt_p, few, block_out)

    grad_normed = normed_stage(proj_p, proj_q, part, piece_p, piece_q)
    rp, rq = fold_cut([blocks(v) for v in rp], core, y), fold_cut([blocks(v) for v in rq], core, x)
    rim = lax.ppermute(grad_normed[:HALO], "seq", [(d + 1, d) for d in range(n_s - 1)])
    (rp, rq), grad_normed, rim = tied((rp, rq), grad_normed, rim)
    both = fold(both, z, F32)[0]
    rp, rq = fold_cut(rp, y, x), fold_cut(rq, x, y)
    grad_in = finish_stage(grad_normed, rim, ext_tok, g, gain_in, rows)
    (rp, rq), grad_in, both = tied((rp, rq), grad_in, both)
    grad_in = home(grad_in)
    w1_grad = cut(jnp.concatenate([fold(rp, x), fold(rq, y)], axis=2), z)
    w1_grad, grad_in, block_out = tied(w1_grad, grad_in, block_out)
    w1_grad = fold(w1_grad, z, F32)[0]
    if aligned:
        small = w1_grad[:8, H:128]
    else:
        small = grad_small_stage(tab_small, gt_p, gt_q, grad_gain_out, few, n_dev, n_s)
        for stage in (core, xy, z):
            small = fold(cut(small, stage), stage, F32)
        small = small[0]
    block_out, grad_in = placed(block_out), placed(grad_in)
    out_wo = jnp.concatenate([both[1, :, :D], both[1, :, D:]], axis=0)
    out_win = jnp.concatenate([both[0], w1_grad[:, FRONT:], w1_grad[:, 128:FRONT], w1_grad[:, :H]], axis=1)
    grad_gain = jnp.sum(out_win * w_in.astype(F32), axis=1) / norm_gain.astype(F32)
    count = dt_bias.shape[0]
    head = lambda k: small[7, k * count : (k + 1) * count]
    return (
        block_out, grad_in, grad_gain, out_win, small[:KERNEL, : conv_b.shape[0]], small[KERNEL, : conv_b.shape[0]],
        head(0), head(1), head(2), small[6, :r_out], out_wo,
    )


def solution(mesh):
    tok = P(None, "fsdp", "seq", None)
    row = P(None, "fsdp", None)
    specs = (tok, row, row, P(BOTH), P(BOTH, None), P(None, BOTH), P(BOTH), P("seq"), P("seq"), P("seq"), P(BOTH), P(BOTH, None), tok)
    outs = (tok, tok, P(BOTH), P(BOTH, None), P(None, BOTH), P(BOTH), P("seq"), P("seq"), P("seq"), P(BOTH), P(BOTH, None))
    return jax.shard_map(body, mesh=mesh, in_specs=specs, out_specs=outs, check_vma=False)
```

```python
import functools

import numpy as np
import jax
import jax.numpy as jnp
from jax import lax
from jax.experimental import pallas as pl
from jax.experimental.pallas import tpu as pltpu
from jax.sharding import PartitionSpec as P

D = 1024
H = 32
P_SIZE = 64
N = 128
KERNEL = 4
MB = 3
INNER = H * P_SIZE
CONV = INNER + 2 * N
HALO = 16
FRONT = 384
TILE = 256
P_TILES = 3
P_COLS = FRONT + P_TILES * TILE
W1_COLS = FRONT + INNER
Q_COLS = W1_COLS - P_COLS
GROUP = 8
EPS = 1e-05
F32 = jnp.float32
BF16 = jnp.bfloat16
BOTH = ("fsdp", "seq")
VMEM = pl.BlockSpec(memory_space=pltpu.VMEM)
SMEM = pl.BlockSpec(memory_space=pltpu.SMEM)
ANY = pl.BlockSpec(memory_space=pl.ANY)
HBM = pl.BlockSpec(memory_space=pltpu.HBM)
SMALL = pl.CostEstimate(flops=1, bytes_accessed=1, transcendentals=0)


def shape(dims, dtype=F32):
    return jax.ShapeDtypeStruct(dims, dtype)


def params(mib=27):
    return pltpu.CompilerParams(vmem_limit_bytes=mib * 2**20)


def permute(block, mask):
    size = lax.axis_size("fsdp") * lax.axis_size("seq")
    return lax.ppermute(block, BOTH, [(i, i ^ mask) for i in range(size)])


def tied(*values):
    return lax.optimization_barrier(values)


def combos(masks):
    found = [0]
    for mask in masks:
        found += [c | mask for c in found]
    return found[1:]


def spread(held, stage):
    return jnp.concatenate([held] + [permute(held, m) for m in stage], axis=0)


def cut(total, stage):
    width = total.shape[0] // (len(stage) + 1)
    return [total[i * width : (i + 1) * width] for i in range(len(stage) + 1)]


def fold(pieces, stage, dtype=BF16):
    total = pieces[0].astype(F32)
    for part, m in zip(pieces[1:], stage):
        total = total + permute(part, m).astype(F32)
    return total.astype(dtype)


def fold_cut(pieces, stage, after):
    parts = [permute(part, m) for part, m in zip(pieces[1:], stage)]
    made = []
    for cuts in zip(*[cut(v, after) for v in [pieces[0]] + parts]):
        total = cuts[0].astype(F32)
        for part in cuts[1:]:
            total = total + part.astype(F32)
        made.append(total.astype(BF16))
    return made


def order_of(stages):
    masks = [0]
    for stage in stages:
        held = list(masks)
        for m in stage:
            masks += [k ^ m for k in held]
    return np.array(masks, np.int32)


def split3(v):
    high = lax.reduce_precision(v, 8, 7)
    mid = lax.reduce_precision(v - high, 8, 7)
    return [p.astype(BF16) for p in (high, mid, v - high - mid)]


def nn(a, b):
    return jnp.dot(a, b, preferred_element_type=F32)


def nt(a, b):
    return lax.dot_general(a, b, (((1,), (1,)), ((), ())), preferred_element_type=F32)


def tn(a, b):
    return lax.dot_general(a, b, (((0,), (0,)), ((), ())), preferred_element_type=F32)


def split(v, count=3):
    parts = []
    for _ in range(count):
        part = v.astype(BF16)
        parts.append(part)
        v = v - part.astype(F32)
    return parts


def one_hot(tile):
    row = lax.broadcasted_iota(jnp.int32, (N, TILE), 0)
    col = lax.broadcasted_iota(jnp.int32, (N, TILE), 1)
    return ((row % H == tile * (TILE // P_SIZE) + col // P_SIZE) & (row < 3 * H)).astype(F32).astype(BF16)


def packed(v):
    lane = lax.broadcasted_iota(jnp.int32, v.shape, 1)
    v = jnp.where(lane < H, v, 0.0)
    high, mid, low = [p.astype(F32) for p in split(v)]
    return (high + pltpu.roll(mid, H, 1) + pltpu.roll(low, 2 * H, 1)).astype(BF16)


def wide(parts, hot):
    return nn(parts, hot)


def head_sum(v, hot):
    return sum(nt(p, hot) for p in split(v, 2))


def sigmoid(v):
    return 1.0 / (1.0 + jnp.exp(-v))


def exact_sum(matrix, v):
    return sum(nn(matrix, p) for p in split(v))


def turned(v):
    return v.astype(F32).T


def block_copies(lin, masks, sources, place, sems):
    copies = []
    half = len(masks) // 2
    for r, mask in enumerate(masks):
        where = lin ^ int(mask)
        source = sources[r // half].at[r % half]
        for src, dst in place(source, where):
            copy = pltpu.make_async_copy(src, dst, sems.at[len(copies)])
            copy.start()
            copies.append(copy)
    return copies


def rows_at(ref, where, height, cols):
    return ref.at[pl.ds(pl.multiple_of(where * height, height), height), cols]


def put(out_ref, piece, offset, width, rows):
    first, shift = offset // 128, offset % 128
    lane = lax.broadcasted_iota(jnp.int32, piece.shape, 1)
    moved = pltpu.roll(jnp.where(lane < width, piece, 0.0), shift, 1) if shift else jnp.where(lane < width, piece, 0.0)
    if shift + width > 128:
        out_ref[rows, first * 128 : first * 128 + 128] += jnp.where(lane >= shift, moved, 0.0)
        out_ref[rows, first * 128 + 128 : first * 128 + 256] += jnp.where(lane < shift, moved, 0.0)
    else:
        out_ref[rows, first * 128 : first * 128 + 128] += moved


def get(in_ref, offset, width, rows):
    first, shift = offset // 128, offset % 128
    piece = in_ref[rows, first * 128 : first * 128 + 128]
    lane = lax.broadcasted_iota(jnp.int32, piece.shape, 1)
    if shift + width > 128:
        piece = jnp.where(lane >= shift, piece, in_ref[rows, first * 128 + 128 : first * 128 + 256])
    piece = pltpu.roll(piece, 128 - shift, 1) if shift else piece
    return jnp.where(lane < width, piece, 0.0)


def small_kernel(n_dev, n_s, total, part, tab, small_ref, line_ref, taps_ref, gin_ref, gout_ref, hp_ref, skip_ref, meta_ref, col_ref, row_ref, conv_s):
    conv_s[...] = jnp.zeros_like(conv_s)
    gin_ref[...] = jnp.zeros_like(gin_ref)
    gout_ref[...] = jnp.zeros_like(gout_ref)
    hp_ref[...] = jnp.zeros_like(hp_ref)
    channels, features, wider, heads = CONV // n_dev, D // n_dev, INNER // n_dev, H // n_s
    everything = slice(0, 8)
    for d in range(n_dev):
        block = small_ref[tab[d]]
        if part:
            block = block.astype(F32)
            block = pltpu.roll(block[:8] + block[8:16] + block[16:24], 128 - H, 1)
        put(conv_s, block, d * channels, channels, everything)
        put(gin_ref, block[5:6], d * features, features, slice(0, 1))
        put(gout_ref, block[6:7], d * wider, wider, slice(0, 1))
        if d < n_s:
            for k in range(3):
                head = block[7:8] if k == 0 else pltpu.roll(block[7:8], 128 - k * heads, 1)
                put(hp_ref, head, d * heads, heads, slice(k, k + 1))
    taps_ref[:, : 2 * N] = conv_s[:, INNER:]
    taps_ref[:, 2 * N :] = conv_s[:, :INNER]
    lane = lax.broadcasted_iota(jnp.int32, (1, N), 1)
    hp_ref[1:2, :] = jnp.where(lane < H, jnp.exp(hp_ref[1:2, :]), 0.0)
    parts = packed(jnp.broadcast_to(hp_ref[2:3, :], (16, N)))
    for j in range(INNER // TILE):
        skip_ref[:, j * TILE : (j + 1) * TILE] = wide(parts, one_hot(j))[:1]
    line = line_ref[...]
    wide_line = line.shape[1]
    moved = lambda v, k: pltpu.roll(v, wide_line - k, 1)[:, :total]
    ids = line[0:1]
    own = moved(ids, HALO)
    keep = lambda test: jnp.where(test, 1.0, 0.0)
    same = [keep(moved(ids, HALO - 3 + k) == own) for k in range(3)]
    before = jnp.sum(jnp.where(lax.broadcasted_iota(jnp.int32, ids.shape, 1) == HALO - 1, ids, 0.0), axis=1, keepdims=True)
    final = jnp.sum(jnp.where(lax.broadcasted_iota(jnp.int32, ids.shape, 1) == HALO + total - 1, ids, 0.0), axis=1, keepdims=True)
    rows = same + [moved(line[1:2], HALO), keep(own == before), keep(own == final), own, own]
    turned_rows = jnp.concatenate(rows, axis=0).T
    meta_ref[...] = turned_rows
    col_ref[...] = turned_rows[:, 6:7]
    row_ref[...] = own


def small_stage(tab, small, line, n_dev, n_s, total):
    return pl.pallas_call(
        functools.partial(small_kernel, n_dev, n_s, total, small.dtype == BF16),
        out_shape=(
            shape((8, CONV)), shape((1, D)), shape((1, INNER)), shape((8, N)), shape((1, INNER)), shape((total, 8)), shape((total, 1)), shape((1, total)),
        ),
        in_specs=[SMEM, VMEM, VMEM],
        out_specs=tuple([VMEM] * 8),
        scratch_shapes=[pltpu.VMEM((8, CONV), F32)],
        compiler_params=params(),
        cost_estimate=SMALL,
        name="small_stage",
    )(tab, small, line)


def grad_small(n_dev, n_s, tab, gp_ref, gq_ref, gout_ref, few_ref, out_ref, conv_s):
    split_at = P_TILES * TILE
    conv_s[:, :split_at] = gp_ref[:, FRONT:]
    conv_s[:, split_at:INNER] = gq_ref[...]
    conv_s[:, INNER:] = gp_ref[:, 128:FRONT]
    channels, wider, heads = CONV // n_dev, INNER // n_dev, H // n_s
    for d in range(n_dev):
        where = (d % n_s) * heads
        head = jnp.zeros((1, 128), F32)
        for k in range(3):
            piece = get(few_ref.at[k], where, heads, slice(0, 1))
            head = head + (pltpu.roll(piece, k * heads, 1) if k else piece)
        rows = [get(conv_s, d * channels, channels, slice(0, 8))[:5], jnp.zeros((1, 128), F32)]
        rows += [get(gout_ref, d * wider, wider, slice(0, 1)), head]
        out_ref[tab[d]] = jnp.concatenate(rows, axis=0)


def grad_small_stage(tab, gp, gq, gout, few, n_dev, n_s):
    return pl.pallas_call(
        functools.partial(grad_small, n_dev, n_s),
        out_shape=shape((n_dev, 8, 128)),
        in_specs=[SMEM] + [VMEM] * 4,
        out_specs=VMEM,
        scratch_shapes=[pltpu.VMEM((8, CONV), F32)],
        compiler_params=params(),
        cost_estimate=SMALL,
        name="grad_small_stage",
    )(tab, gp, gq, gout, few)


def weight_copies(lin, masks_p, masks_q, po, px, qo, qx, w1_s, sem_p, sem_q):
    rows = D // len(masks_p)
    place = lambda cols: lambda src, where: [(src, rows_at(w1_s, where, rows, cols))]
    first = block_copies(lin, masks_p, (po, px), place(pl.ds(0, P_COLS)), sem_p)
    second = block_copies(lin, masks_q, (qo, qx), place(pl.ds(P_COLS, Q_COLS)), sem_q)
    return first, second


def first_kernel(masks_p, masks_q, total, lin_ref, halo_ref, t0_ref, t1_ref, t2_ref, gain_ref, meta_ref, taps_ref, hp_ref, po, px, qo, qx,
                 normed_ref, cin_ref, pre_ref, bc_ref, x_ref, dtx_ref, hd_ref, cumt_ref, pay_ref, cin_s, w1_s, cin_b, pre_b, sem_p, sem_q, sem_out):
    first, second = weight_copies(lin_ref[0], masks_p, masks_q, po, px, qo, qx, w1_s, sem_p, sem_q)
    start = 0
    for ref in (halo_ref, t0_ref, t1_ref, t2_ref):
        u = ref[...].astype(F32)
        scale = lax.rsqrt(jnp.mean(u * u, axis=-1, keepdims=True) + EPS)
        normed_ref[start : start + u.shape[0], :] = (u * scale * gain_ref[...]).astype(BF16)
        start += u.shape[0]
    written = []

    def write(source, target):
        copy = pltpu.make_async_copy(source, target, sem_out.at[len(written)])
        copy.start()
        written.append(copy)

    for copy in first:
        copy.wait()
    meta = meta_ref[...]
    same = [meta[:, k : k + 1] for k in range(3)]
    valid, carry, tail = meta[:, 3:4], meta[:, 4:5], meta[:, 5:6]

    def conv(made, cols):
        cin_s[...] = made
        cin_b[:, cols] = made.astype(BF16)
        acc = taps_ref[4:5, cols] + taps_ref[3:4, cols] * made[HALO:]
        for k in range(3):
            acc = acc + taps_ref[k : k + 1, cols] * (cin_s[HALO - 3 + k : HALO - 3 + k + total, :] * same[k])
        pre_b[:, cols] = acc.astype(BF16)
        write(cin_b.at[:, cols], cin_ref.at[:, cols])
        write(pre_b.at[:, cols], pre_ref.at[:, cols])
        return (acc * sigmoid(acc)).astype(BF16)

    front = nn(normed_ref[...], w1_s[:, :FRONT])
    lane = lax.broadcasted_iota(jnp.int32, (total, 128), 1)
    shifted = jnp.where(lane < H, front[HALO:, :128], 0.0).astype(BF16).astype(F32) + hp_ref[0:1, :]
    dt = (jnp.maximum(shifted, 0.0) + jnp.log1p(jnp.exp(-jnp.abs(shifted)))) * valid
    row = lax.broadcasted_iota(jnp.int32, (total, total), 0)
    col = lax.broadcasted_iota(jnp.int32, (total, total), 1)
    lower = (row >= col).astype(F32).astype(BF16)
    cum = exact_sum(lower, -dt * hp_ref[1:2, :])
    reach = jnp.exp(cum) * carry
    w_end = jnp.exp(cum[total - 1 : total] - cum) * tail
    hd_ref[0], hd_ref[1], hd_ref[2], hd_ref[3], hd_ref[4] = dt, cum, reach, w_end, shifted
    cumt_ref[...] = cum.T[:H]
    bc = conv(front[:, 128:], pl.ds(0, 2 * N))
    bc_ref[...] = bc
    b_turned = turned(bc[:, :N]).astype(BF16)
    through = jnp.broadcast_to(reach[total - 1 : total], (8, N))
    dt_parts, both_parts = packed(dt), packed(dt * w_end)
    through_parts = [packed(p.astype(F32)) for p in split(through)]
    for j in range(INNER // TILE):
        if j == P_TILES:
            for copy in second:
                copy.wait()
        cols = pl.ds(2 * N + j * TILE, TILE)
        own = slice(j * TILE, (j + 1) * TILE)
        x = conv(nn(normed_ref[...], w1_s[:, FRONT + j * TILE : FRONT + (j + 1) * TILE]), cols)
        x_ref[:, own] = x
        xf = x.astype(F32)
        hot = one_hot(j)
        dtx_ref[:, own] = (xf * wide(dt_parts, hot)).astype(BF16)
        pay_ref[:N, own] = nn(b_turned, (xf * wide(both_parts, hot)).astype(BF16)).astype(BF16)
        extra = [nn(p, hot)[:1] for p in through_parts]
        pay_ref[N:, own] = jnp.concatenate(extra + [jnp.zeros((HALO - 3, TILE), F32)], axis=0).astype(BF16)
    for copy in written:
        copy.wait()


def first_stage(tok, gain_in, meta, taps, hp, p, q, total):
    (po, px, masks_p, lin_p), (qo, qx, masks_q, _) = p, q
    ext = total + HALO
    return pl.pallas_call(
        functools.partial(first_kernel, masks_p, masks_q, total),
        out_shape=(
            shape((ext, D), BF16), shape((ext, CONV), BF16), shape((total, CONV), BF16), shape((total, 2 * N), BF16),
            shape((total, INNER), BF16), shape((total, INNER), BF16), shape((5, total, N)), shape((H, total)), shape((N + HALO, INNER), BF16),
        ),
        in_specs=[SMEM] + [VMEM] * 8 + [ANY] * 4,
        out_specs=(VMEM, HBM, HBM) + tuple([VMEM] * 6),
        scratch_shapes=[pltpu.VMEM((ext, TILE), F32), pltpu.VMEM((D, W1_COLS), BF16), pltpu.VMEM((ext, CONV), BF16), pltpu.VMEM((total, CONV), BF16), pltpu.SemaphoreType.DMA((len(masks_p),)), pltpu.SemaphoreType.DMA((len(masks_q),)), pltpu.SemaphoreType.DMA((2 * (INNER // TILE + 1),))],
        compiler_params=params(),
        cost_estimate=SMALL,
        name="first_stage",
    )(lin_p, *tok, gain_in, meta, taps, hp, po, px, qo, qx)


def late_copies(count, blocks, wg_s, wo_s, sem_g, sem_o):
    rows = D // count
    first, second = [], []
    for r in range(count):
        copy = pltpu.make_async_copy(blocks.at[r, 0], wg_s.at[pl.ds(r * rows, rows)], sem_g.at[r])
        copy.start()
        first.append(copy)
    for r in range(count):
        for i in range(2):
            target = wo_s.at[pl.ds((2 * r + i) * rows, rows)]
            copy = pltpu.make_async_copy(blocks.at[r, 1, :, pl.ds(i * D, D)], target, sem_o.at[2 * r + i])
            copy.start()
            second.append(copy)
    return first, second


def late_scratch(count):
    return [pltpu.VMEM((D, INNER), BF16), pltpu.VMEM((INNER, D), BF16), pltpu.SemaphoreType.DMA((count,)), pltpu.SemaphoreType.DMA((2 * count,))]


def gate_kernel(count, normed_ref, g_ref, blocks, ga_ref, dga_ref, gno_ref, wg_s, wo_s, sem_g, sem_o):
    first, second = late_copies(count, blocks, wg_s, wo_s, sem_g, sem_o)
    for copy in first:
        copy.wait()
    for j in range(INNER // TILE):
        own = slice(j * TILE, (j + 1) * TILE)
        gate = nn(normed_ref[HALO:], wg_s[:, own])
        sig = sigmoid(gate)
        ga_ref[:, own] = (gate * sig).astype(BF16)
        dga_ref[:, own] = (sig * (1.0 + gate * (1.0 - sig))).astype(BF16)
    for copy in second:
        copy.wait()
    for j in range(INNER // TILE):
        own = slice(j * TILE, (j + 1) * TILE)
        gno_ref[:, own] = nt(g_ref[...], wo_s[own, :]).astype(BF16)


def gate_stage(normed, g, blocks, total):
    count = blocks.shape[0]
    return pl.pallas_call(
        functools.partial(gate_kernel, count),
        out_shape=(shape((total, INNER), BF16),) * 3,
        in_specs=[VMEM] * 2 + [HBM],
        out_specs=tuple([VMEM] * 3),
        scratch_shapes=late_scratch(count),
        compiler_params=params(40),
        cost_estimate=SMALL,
        name="gate_stage",
    )(normed, g, blocks)


def left_lanes():
    return lax.broadcasted_iota(jnp.int32, (1, 2 * P_SIZE), 1) < P_SIZE


def pairs_kernel(total, bc_ref, dtx_ref, cumt_ref, id_col, id_row, out_ref, cb_ref, mask_ref):
    @pl.when(pl.program_id(0) == 0)
    def _():
        cb_ref[...] = nt(bc_ref[:, N:], bc_ref[:, :N])
        row = lax.broadcasted_iota(jnp.int32, (total, total), 0)
        col = lax.broadcasted_iota(jnp.int32, (total, total), 1)
        mask_ref[...] = jnp.where((row >= col) & (id_col[...] == id_row[...]), 0.0, -1e30)

    cum_cols = cumt_ref[...].T
    left = left_lanes()
    for pair in range(GROUP // 2):
        lanes = slice(pair * 2 * P_SIZE, (pair + 1) * 2 * P_SIZE)
        for a in range(total // N):
            rows, width = slice(a * N, (a + 1) * N), (a + 1) * N
            made = []
            for i in (2 * pair, 2 * pair + 1):
                decay = jnp.exp(cum_cols[rows, i : i + 1] - cumt_ref[i : i + 1, :width] + mask_ref[rows, :width])
                made.append(nn((decay * cb_ref[rows, :width]).astype(BF16), dtx_ref[:width, lanes]))
            out_ref[rows, lanes] = jnp.where(left, made[0], made[1])


def pairs_stage(bc, dtx, cumt, id_col, id_row, total):
    block = pl.BlockSpec((total, GROUP * P_SIZE), lambda g: (0, g))
    return pl.pallas_call(
        functools.partial(pairs_kernel, total),
        grid=(H // GROUP,),
        out_shape=shape((total, INNER)),
        in_specs=[VMEM, block, pl.BlockSpec((GROUP, total), lambda g: (g, 0)), VMEM, VMEM],
        out_specs=block,
        scratch_shapes=[pltpu.VMEM((total, total), F32)] * 2,
        compiler_params=params(),
        cost_estimate=SMALL,
        name="pairs_stage",
    )(bc, dtx, cumt, id_col, id_row)


def pairs_back_kernel(total, bc_ref, dtx_ref, e_ref, cumt_ref, id_col, id_row, gdtx_ref, gb_ref, gc_ref, cb_ref, mask_ref, acc_ref):
    @pl.when(pl.program_id(0) == 0)
    def _():
        cb_ref[...] = nt(bc_ref[:, :N], bc_ref[:, N:])
        row = lax.broadcasted_iota(jnp.int32, (total, total), 0)
        col = lax.broadcasted_iota(jnp.int32, (total, total), 1)
        mask_ref[...] = jnp.where((row <= col) & (id_col[...] == id_row[...]), 0.0, -1e30)
        acc_ref[...] = jnp.zeros_like(acc_ref)

    cum_cols = cumt_ref[...].T
    left = left_lanes()
    for pair in range(GROUP // 2):
        lanes = slice(pair * 2 * P_SIZE, (pair + 1) * 2 * P_SIZE)
        for a in range(total // N):
            rows, after = slice(a * N, (a + 1) * N), slice(a * N, total)
            made, added = [], None
            for side, i in enumerate((2 * pair, 2 * pair + 1)):
                decay = jnp.exp(cumt_ref[i : i + 1, after] - cum_cols[rows, i : i + 1] + mask_ref[rows, after])
                made.append(nn((decay * cb_ref[rows, after]).astype(BF16), e_ref[after, lanes]))
                mine = dtx_ref[rows, lanes].astype(F32)
                mine = jnp.where(left, mine, 0.0) if side == 0 else jnp.where(left, 0.0, mine)
                term = nt(mine.astype(BF16), e_ref[after, lanes]) * decay
                added = term if added is None else added + term
            gdtx_ref[rows, lanes] = jnp.where(left, made[0], made[1])
            acc_ref[rows, after] += added

    @pl.when(pl.program_id(0) == H // GROUP - 1)
    def _():
        gb_ref[...] = nn(acc_ref[...].astype(BF16), bc_ref[:, N:])
        gc_ref[...] = nn(acc_ref[...].T.astype(BF16), bc_ref[:, :N])


def pairs_back_stage(bc, dtx, e, cumt, id_col, id_row, total):
    block = pl.BlockSpec((total, GROUP * P_SIZE), lambda g: (0, g))
    flat = pl.BlockSpec((total, N), lambda g: (0, 0))
    return pl.pallas_call(
        functools.partial(pairs_back_kernel, total),
        grid=(H // GROUP,),
        out_shape=(shape((total, INNER)), shape((total, N)), shape((total, N))),
        in_specs=[VMEM, block, block, pl.BlockSpec((GROUP, total), lambda g: (g, 0)), VMEM, VMEM],
        out_specs=(block, flat, flat),
        scratch_shapes=[pltpu.VMEM((total, total), F32)] * 3,
        compiler_params=params(),
        cost_estimate=SMALL,
        name="pairs_back_stage",
    )(bc, dtx, e, cumt, id_col, id_row)


def combined(refs, cols):
    states = refs[0][:N, cols].astype(F32)
    factor = None
    for near, ref in zip(refs, refs[1:]):
        step = jnp.sum(near[N:, cols].astype(F32), axis=0, keepdims=True)
        factor = step if factor is None else factor * step
        states = states + factor * ref[:N, cols].astype(F32)
    return states


def double_kernel(own_ref, next_ref, out_ref):
    for j in range(INNER // TILE):
        cols = slice(j * TILE, (j + 1) * TILE)
        factor = jnp.sum(own_ref[N:, cols].astype(F32), axis=0, keepdims=True)
        further = jnp.sum(next_ref[N:, cols].astype(F32), axis=0, keepdims=True)
        out_ref[:N, cols] = (own_ref[:N, cols].astype(F32) + factor * next_ref[:N, cols].astype(F32)).astype(BF16)
        parts = [p.astype(F32) for p in split(factor * further)]
        out_ref[N:, cols] = jnp.concatenate(parts + [jnp.zeros((HALO - 3, TILE), F32)], axis=0).astype(BF16)


def double_stage(own, following):
    return pl.pallas_call(
        double_kernel,
        out_shape=shape(own.shape, BF16),
        in_specs=[VMEM] * 2,
        out_specs=VMEM,
        compiler_params=params(),
        cost_estimate=SMALL,
        name="double_stage",
    )(own, following)


def output_kernel(count, total, *refs):
    got = refs[:count]
    (inside_ref, bc_ref, x_ref, hd_ref, ga_ref, dga_ref, gno_ref, gain_ref, skip_ref, own_ref,
     state_ref, no_ref, e_ref, gg_ref, pay_ref, gc_ref, rows_ref, ggain_ref, scan_s, gated_s) = refs[count:]
    c_part = bc_ref[:, N:]
    reach = packed(hd_ref[2])
    squares = jnp.zeros((total, 1), F32)
    crossed = jnp.zeros((total, 1), F32)
    for j in range(INNER // TILE):
        own = slice(j * TILE, (j + 1) * TILE)
        state = combined(got, own).astype(BF16)
        state_ref[:, own] = state
        scan = inside_ref[:, own] + nn(c_part, state) * wide(reach, one_hot(j))
        scan_s[:, own] = scan
        mixed = (scan + skip_ref[:, own] * x_ref[:, own].astype(F32)).astype(BF16)
        gg_ref[:, own] = mixed
        gated = mixed.astype(F32) * ga_ref[:, own].astype(F32)
        gated_s[:, own] = gated
        squares = squares + jnp.sum(gated * gated, axis=-1, keepdims=True)
        crossed = crossed + jnp.sum(gno_ref[:, own].astype(F32) * gain_ref[:, own] * gated, axis=-1, keepdims=True)
    scale = lax.rsqrt(squares / INNER + EPS)
    mean = crossed * scale / INNER
    c_turned = turned(c_part).astype(BF16)
    grad_c = jnp.zeros((total, N), F32)
    row_sum = jnp.zeros((total, N), F32)
    for j in range(INNER // TILE):
        own = slice(j * TILE, (j + 1) * TILE)
        hot = one_hot(j)
        unit = gated_s[:, own] * scale
        gno = gno_ref[:, own].astype(F32)
        no_ref[:, own] = (unit * gain_ref[:, own]).astype(BF16)
        ggain_ref[:, own] = jnp.sum(gno * unit, axis=0, keepdims=True)
        grad = scale * (gno * gain_ref[:, own] - unit * mean)
        e = (grad * ga_ref[:, own].astype(F32)).astype(BF16)
        e_ref[:, own] = e
        gg_ref[:, own] = (grad * gg_ref[:, own].astype(F32) * dga_ref[:, own].astype(F32)).astype(BF16)
        ef = e.astype(F32)
        e_reach = (ef * wide(reach, hot)).astype(BF16)
        pay_ref[:N, own] = nn(c_turned, e_reach).astype(BF16)
        grad_c = grad_c + nt(e_reach, state_ref[:, own])
        row_sum = row_sum + head_sum(ef * scan_s[:, own], hot)
    pay_ref[N:, :] = own_ref[N:, :]
    gc_ref[...] = grad_c
    rows_ref[...] = row_sum


def output_stage(got, inside, bc, x, hd, ga, dga, gno, gain_out, skip_wide, pay, total):
    count = len(got)
    big = lambda t: shape((total, INNER), t)
    return pl.pallas_call(
        functools.partial(output_kernel, count, total),
        out_shape=(shape((N, INNER), BF16), big(BF16), big(BF16), big(BF16), shape((N + HALO, INNER), BF16), shape((total, N)), shape((total, N)), shape((1, INNER))),
        in_specs=[VMEM] * (count + 10),
        out_specs=tuple([VMEM] * 8),
        scratch_shapes=[pltpu.VMEM((total, INNER), F32)] * 2,
        compiler_params=params(),
        cost_estimate=SMALL,
        name="output_stage",
    )(*got, inside, bc, x, hd, ga, dga, gno, gain_out, skip_wide, pay)


def turn_kernel(count, tab_p, tab_q, normed_ref, p_ref, q_ref):
    rows = D // count
    for j in range(D // TILE):
        made = normed_ref[:, j * TILE : (j + 1) * TILE].astype(F32).T.astype(BF16)
        for i in range(TILE // rows):
            block = made[i * rows : (i + 1) * rows]
            a = j * (TILE // rows) + i
            p_ref[pl.ds(pl.multiple_of(tab_p[a] * rows, rows), rows), :] = block
            q_ref[pl.ds(pl.multiple_of(tab_q[a] * rows, rows), rows), :] = block


def turn_stage(tab_p, tab_q, normed):
    out = shape((D, normed.shape[0]), BF16)
    return pl.pallas_call(
        functools.partial(turn_kernel, tab_p.shape[0]),
        out_shape=(out, out),
        in_specs=[SMEM, SMEM, VMEM],
        out_specs=(VMEM, VMEM),
        compiler_params=params(),
        cost_estimate=SMALL,
        name="turn_stage",
    )(tab_p, tab_q, normed)


def weights_kernel(count, tab_q, turned_ref, gg_ref, no_ref, g_ref, keep_g, send_g, keep_o, send_o, turned_s):
    for j in range(INNER // TILE):
        own = slice(j * TILE, (j + 1) * TILE)
        weight_grad(turned_ref[:, HALO:], gg_ref[:, own], own, keep_g, send_g)
    rows = INNER // count
    for j in range(INNER // TILE):
        made = no_ref[:, j * TILE : (j + 1) * TILE].astype(F32).T.astype(BF16)
        for i in range(TILE // rows):
            place = pl.ds(pl.multiple_of(tab_q[j * (TILE // rows) + i] * rows, rows), rows)
            turned_s[place, :] = made[i * rows : (i + 1) * rows]
    for j in range(D // TILE):
        own = slice(j * TILE, (j + 1) * TILE)
        weight_grad(turned_s[...], g_ref[:, own], own, keep_o, send_o)


def weights_stage(tab_q, turned_rows, grad_gate, normed_out, g, total):
    return pl.pallas_call(
        functools.partial(weights_kernel, tab_q.shape[0]),
        out_shape=(shape((D // 2, INNER), BF16),) * 2 + (shape((D, D), BF16),) * 2,
        in_specs=[SMEM] + [VMEM] * 4,
        out_specs=tuple([VMEM] * 4),
        scratch_shapes=[pltpu.VMEM((INNER, total), BF16)],
        compiler_params=params(),
        cost_estimate=SMALL,
        name="weights_stage",
    )(tab_q, turned_rows, grad_gate, normed_out, g)


def rest_kernel(count, no_ref, gg_ref, tok_ref, blocks, out_ref, part_ref, wg_s, wo_s, sem_g, sem_o):
    first, second = late_copies(count, blocks, wg_s, wo_s, sem_g, sem_o)
    for copy in first:
        copy.wait()
    half = D // 4
    for j in range(4):
        own = slice(j * half, (j + 1) * half)
        part_ref[:, own] = nt(gg_ref[...], wg_s[own, :])
    for copy in second:
        copy.wait()
    for j in range(4):
        own = slice(j * half, (j + 1) * half)
        out_ref[:, own] = (tok_ref[HALO:, own].astype(F32) + nn(no_ref[...], wo_s[:, own])).astype(BF16)


def rest_stage(normed_out, grad_gate, ext_tok, blocks, total):
    count = blocks.shape[0]
    return pl.pallas_call(
        functools.partial(rest_kernel, count),
        out_shape=(shape((total, D), BF16), shape((total, D))),
        in_specs=[VMEM] * 3 + [HBM],
        out_specs=(VMEM, VMEM),
        scratch_shapes=late_scratch(count),
        compiler_params=params(40),
        cost_estimate=SMALL,
        name="rest_stage",
    )(normed_out, grad_gate, ext_tok, blocks)


def heads_back(count, total, tiles, got, refs, sums, emit):
    gdtx_ref, e_ref, x_ref, dtx_ref, bc_ref, state_ref, hd_ref, skip_ref = refs
    gb, q_sum, back_sum, xg, both, gskip = sums
    b_part = bc_ref[:, :N]
    dt_parts, end_parts = packed(hd_ref[0]), packed(hd_ref[3])
    for n, j in enumerate(tiles):
        own = slice(j * TILE, (j + 1) * TILE)
        hot = one_hot(j)
        later = combined(got, own)
        later_low = later.astype(BF16)
        w_end, dt = wide(end_parts, hot), wide(dt_parts, hot)
        from_later = nn(b_part, later_low) * w_end
        inner = gdtx_ref[:, own]
        dtx = dtx_ref[:, own].astype(F32)
        x, e = x_ref[:, own].astype(F32), e_ref[:, own].astype(F32)
        q_sum = q_sum + head_sum(dtx * from_later, hot)
        back_sum = back_sum + head_sum(dtx * inner, hot)
        grad = inner + from_later
        xg = xg + head_sum(x * grad, hot)
        crossing = jnp.sum(state_ref[:, own].astype(F32) * later, axis=0, keepdims=True)
        skipped = jnp.sum(x * e, axis=0, keepdims=True)
        both = both + head_sum(jnp.broadcast_to(crossing, (8, TILE)), hot)
        gskip = gskip + head_sum(jnp.broadcast_to(skipped, (8, TILE)), hot)
        gb = gb + nt((dtx * w_end).astype(BF16), later_low)
        emit(n, j, (dt * grad + skip_ref[:, own] * e).astype(BF16).astype(F32))
    return gb, q_sum, back_sum, xg, both, gskip


def conv_back(total, grad_act, cols, place, conv_refs, ext_s, cin_s):
    pre_ref, cin_ref, taps_ref, meta_ref, gt_ref = conv_refs
    pre = pre_ref[:, cols].astype(F32)
    sig = sigmoid(pre)
    cin_s[...] = cin_ref[:, cols].astype(F32)
    grad = grad_act * sig * (1.0 + pre * (1.0 - sig))
    gt_ref[KERNEL : KERNEL + 1, place] = jnp.sum(grad, axis=0, keepdims=True)
    ext_s[...] = jnp.zeros_like(ext_s)
    for k in range(KERNEL):
        masked = grad if k == 3 else grad * meta_ref[:, k : k + 1]
        rows = slice(HALO - 3 + k, HALO - 3 + k + total)
        gt_ref[k : k + 1, place] = jnp.sum(masked * cin_s[rows, :], axis=0, keepdims=True)
        ext_s[rows, :] += masked * taps_ref[k : k + 1, cols]
    return ext_s[...].astype(BF16)


def weight_grad(turned, grads, place, keep_ref, send_ref):
    made = nn(turned, grads)
    half = made.shape[0] // 2
    keep_ref[:, place] = made[:half].astype(BF16)
    send_ref[:, place] = made[half:].astype(BF16)


def back_kernel(count, total, last, small, *refs):
    got, refs = refs[:count], refs[count:]
    heads, refs = refs[:8], refs[8:]
    pre_ref, cin_ref, taps_ref, meta_ref, turned_ref = refs[:5]
    refs = refs[5:]
    if last:
        acc_in, few_in, gcs_ref, gcp_ref, gbp_ref, rows_ref, hp_ref = refs[:7]
        refs = refs[7:]
        if small:
            gt_first, gout_ref, tab = refs[:3]
            refs = refs[3:]
    keep_ref, send_ref, proj_ref, gt_ref, acc_ref, few_ref, ext_s, cin_s = refs[:8]
    conv_refs = (pre_ref, cin_ref, taps_ref, meta_ref, gt_ref)
    gt_ref[...] = jnp.zeros_like(gt_ref)
    base = FRONT if last else 0

    def emit(n, j, grad_x):
        place = slice(base + n * TILE, base + (n + 1) * TILE)
        grads = conv_back(total, grad_x, slice(2 * N + j * TILE, 2 * N + (j + 1) * TILE), place, conv_refs, ext_s, cin_s)
        proj_ref[:, place] = grads
        weight_grad(turned_ref[...], grads, place, keep_ref, send_ref)

    tiles = range(P_TILES) if last else range(P_TILES, INNER // TILE)
    if last:
        sums = tuple(acc_in[i] for i in range(4)) + (few_in[0], few_in[1])
    else:
        zero = jnp.zeros((total, N), F32)
        sums = (zero,) * 4 + (jnp.zeros((8, N), F32),) * 2
    gb, q_sum, back_sum, xg, both, gskip = heads_back(count, total, tiles, got, heads, sums, emit)
    if not last:
        acc_ref[0], acc_ref[1], acc_ref[2], acc_ref[3] = gb, q_sum, back_sum, xg
        few_ref[0], few_ref[1] = both, gskip
        return
    hd_ref = heads[6]
    grad_bc = jnp.concatenate([gb + gbp_ref[...], gcs_ref[...] + gcp_ref[...]], axis=1)
    place = slice(128, FRONT)
    proj_ref[:, place] = conv_back(total, grad_bc, slice(0, 2 * N), place, conv_refs, ext_s, cin_s)
    row = lax.broadcasted_iota(jnp.int32, (total, total), 0)
    col = lax.broadcasted_iota(jnp.int32, (total, total), 1)
    upper = (row <= col).astype(F32).astype(BF16)
    below = (row > col).astype(F32).astype(BF16)
    dt, reach, shifted, rate = hd_ref[0], hd_ref[2], hd_ref[4], hp_ref[1:2, :]
    grad_ld = exact_sum(upper, rows_ref[...] - back_sum) + exact_sum(below, q_sum) + both[0:1] * reach[total - 1 : total]
    grad_step = (xg - grad_ld * rate) * meta_ref[:, 3:4] * sigmoid(shifted)
    grad_step = jnp.where(lax.broadcasted_iota(jnp.int32, grad_step.shape, 1) < H, grad_step, 0.0)
    proj_ref[:HALO, :128] = jnp.zeros((HALO, 128), BF16)
    proj_ref[HALO:, :128] = grad_step.astype(BF16)
    few_ref[0] = jnp.broadcast_to(jnp.sum(grad_step, axis=0, keepdims=True), (8, N))
    few_ref[1] = jnp.broadcast_to(jnp.sum(grad_ld * (-dt * rate), axis=0, keepdims=True), (8, N))
    few_ref[2] = gskip
    acc_ref[...] = jnp.zeros_like(acc_ref)
    if not small:
        weight_grad(turned_ref[...], proj_ref[:, :FRONT], slice(0, FRONT), keep_ref, send_ref)
        return
    small_s, front_s, conv_s = refs[8:]
    grad_small(*small, tab, gt_ref, gt_first, gout_ref, few_ref, small_s, conv_s)
    made = nn(turned_ref[...], proj_ref[:, :FRONT])
    front_s[...] = made[:, :128]
    rows = D // small[0]
    for r in range(small[0]):
        front_s[r * rows : r * rows + 8, :] += pltpu.roll(small_s[r], H, 1)
    half = D // 2
    keep_ref[:, :128], send_ref[:, :128] = front_s[:half].astype(BF16), front_s[half:].astype(BF16)
    keep_ref[:, 128:FRONT], send_ref[:, 128:FRONT] = made[:half, 128:].astype(BF16), made[half:, 128:].astype(BF16)


def back_stage(got, heads, conv_refs, turned_rows, more, total, small=()):
    last = bool(more)
    width = P_COLS if last else Q_COLS
    ext = total + HALO
    acc = shape((1, 8, N)) if last else shape((4, total, N))
    scratch = [pltpu.VMEM((ext, TILE), F32)] * 2
    if small:
        scratch += [pltpu.VMEM((small[0], 8, 128), F32), pltpu.VMEM((D, 128), F32), pltpu.VMEM((8, CONV), F32)]
    return pl.pallas_call(
        functools.partial(back_kernel, len(got), total, last, small),
        out_shape=(shape((D // 2, width), BF16), shape((D // 2, width), BF16), shape((ext, width), BF16), shape((8, width)), acc, shape((3 if last else 2, 8, N))),
        in_specs=[VMEM] * (len(got) + 13 + len(more) - bool(small)) + [SMEM] * bool(small),
        out_specs=tuple([VMEM] * 6),
        scratch_shapes=scratch,
        compiler_params=params(),
        cost_estimate=SMALL,
        name="back_last" if last else "back_first",
    )(*got, *heads, *conv_refs, turned_rows, *more)


def normed_kernel(masks_p, masks_q, lin_ref, pp_ref, pq_ref, part_ref, po, px, qo, qx, out_ref, w1_s, sem_p, sem_q):
    first, second = weight_copies(lin_ref[0], masks_p, masks_q, po, px, qo, qx, w1_s, sem_p, sem_q)
    for copy in first + second:
        copy.wait()
    out_ref[...] = nt(pp_ref[:, 128:], w1_s[:, 128:P_COLS]) + nt(pq_ref[...], w1_s[:, P_COLS:])
    out_ref[...] += nt(pp_ref[:, :H], w1_s[:, :H])
    out_ref[HALO:, :] += part_ref[...]


def normed_stage(proj_p, proj_q, part, p, q):
    (po, px, masks_p, lin), (qo, qx, masks_q, _) = p, q
    return pl.pallas_call(
        functools.partial(normed_kernel, masks_p, masks_q),
        out_shape=shape((proj_p.shape[0], D)),
        in_specs=[SMEM] + [VMEM] * 3 + [ANY] * 4,
        out_specs=VMEM,
        scratch_shapes=[pltpu.VMEM((D, W1_COLS), BF16), pltpu.SemaphoreType.DMA((len(masks_p),)), pltpu.SemaphoreType.DMA((len(masks_q),))],
        compiler_params=params(),
        cost_estimate=SMALL,
        name="normed_stage",
    )(lin, proj_p, proj_q, part, po, px, qo, qx)


def finish_kernel(normed_ref, rim_ref, tok_ref, g_ref, gain_ref, *outs):
    rows = outs[0].shape[0]
    for i, out_ref in enumerate(outs):
        own = slice(HALO + i * rows, HALO + (i + 1) * rows)
        u = tok_ref[own, :].astype(F32)
        scale = lax.rsqrt(jnp.mean(u * u, axis=-1, keepdims=True) + EPS)
        grad = normed_ref[own, :]
        if i == len(outs) - 1:
            grad = jnp.concatenate([grad[: rows - HALO], grad[rows - HALO :] + rim_ref[...]], axis=0)
        unit, q = u * scale, grad * gain_ref[...]
        out_ref[...] = (g_ref[i * rows : (i + 1) * rows, :].astype(F32) + scale * (q - unit * jnp.mean(q * unit, axis=-1, keepdims=True))).astype(BF16)


def finish_stage(grad_normed, rim, ext_tok, g, gain_in, rows):
    return pl.pallas_call(
        finish_kernel,
        out_shape=(shape((rows, D), BF16),) * MB,
        in_specs=[VMEM] * 5,
        out_specs=tuple([VMEM] * MB),
        compiler_params=params(),
        cost_estimate=SMALL,
        name="finish_stage",
    )(grad_normed, rim, ext_tok, g, gain_in)


def body(tokens, scene_ids, valid_mask, norm_gain, w_in, conv_w, conv_b, dt_bias, a_log, d_skip, gate_gain, w_out, d_out):
    n_f, n_s = lax.axis_size("fsdp"), lax.axis_size("seq")
    n_dev = n_f * n_s
    s_rank = lax.axis_index("seq")
    lin = lax.axis_index("fsdp") * n_s + s_rank
    rows = tokens.shape[2]
    total, length = MB * rows, n_s * rows
    r_in, r_out = w_in.shape[0], w_out.shape[0]
    f_bits = [n_s << b for b in range(n_f.bit_length() - 1)]
    s_bits = [1 << b for b in range(n_s.bit_length() - 1)]
    n_x = len(f_bits) - 1
    z, x, y = combos(s_bits[n_x:]), combos(s_bits[:n_x]), combos(f_bits[1:])
    xy, core = combos(s_bits[:n_x] + f_bits[1:]), [n_s]
    orders = [order_of([z, x, y, core]), order_of([z, y, x, core]), order_of([z, xy, core])]
    aligned = r_in % 16 == 0
    tables = jnp.asarray(np.stack([np.argsort(o) for o in orders]), jnp.int32)[:, jnp.arange(n_dev) ^ lin]

    inverse3 = pow(3, -1, n_s)
    source = lambda i: [((3 * d + i) % n_s, d) for d in range(n_s)]

    def chosen(arr, i):
        d = (inverse3 * (s_rank - i + n_s)) % n_s
        return lax.select_n((3 * d + i + MB * n_s) // n_s % MB, arr[0, 0], arr[1, 0], arr[2, 0])

    def home(parts):
        return [lax.ppermute(part, "seq", [(d, k) for k, d in source(i)]) for i, part in enumerate(parts)]

    def placed(blocks):
        return jnp.stack([lax.select_n((m * n_s + s_rank) % MB, *blocks) for m in range(MB)])[:, None]

    late = jnp.concatenate([w_in[:, :INNER], jnp.concatenate([w_out[: r_out // 2], w_out[r_out // 2 :]], axis=1)])
    spare = 128 - H
    line = lambda v: jnp.pad(v.astype(F32), ((0, 0), (0, (spare if aligned else 128) - v.shape[1])))
    heads = jnp.concatenate([dt_bias, a_log, d_skip])[None]
    small = jnp.concatenate([line(conv_w), line(conv_b[None]), line(norm_gain[None]), line(gate_gain[None]), line(heads)])
    if aligned:
        pad = jnp.pad(jnp.concatenate(split3(small)), ((0, r_in - 24), (0, 0)))
    else:
        pad = jnp.zeros((r_in, spare), BF16)
    w1 = jnp.concatenate([w_in[:, INNER + CONV :], pad, w_in[:, 2 * INNER : INNER + CONV], w_in[:, INNER : 2 * INNER]], axis=1)

    first = spread(w1[None], z)
    halo = lax.ppermute(chosen(tokens, -1)[rows - HALO :], "seq", source(-1))
    first, halo, tokens, d_out, tables = tied(first, halo, tokens, d_out, tables)
    tab_small = tables[2]
    tab_p, tab_q = (tables[0], tables[1]) if aligned else (jnp.arange(32, dtype=jnp.int32),) * 2
    p, q = first[..., :P_COLS], first[..., P_COLS:]
    got = [lax.ppermute(chosen(tokens, i), "seq", source(i)) for i in range(MB)]
    picked = [chosen(d_out, i) for i in range(MB)]
    p, q, picked = tied(spread(p, x), spread(q, y), picked)
    ids = (scene_ids[:, 0] + 8 * jnp.arange(MB, dtype=jnp.int32)[:, None]).reshape(1, -1)
    lines = jnp.concatenate([jnp.pad(ids, ((0, 0), (HALO, 0)), constant_values=-1), jnp.pad(valid_mask[:, 0].reshape(1, -1), ((0, 0), (HALO, 0)))])
    lines = lax.dynamic_slice_in_dim(lines, s_rank * total, total + HALO, axis=1)
    lines = jnp.pad(lines.astype(F32), ((0, 6), (0, -(total + HALO) % 128)))
    p, q, lines, picked, *got = tied(spread(p, y), spread(q, x), lines, picked, *got)
    g = [lax.ppermute(picked[i], "seq", source(i)) for i in range(MB)]
    p_other, q_other = permute(p, n_s), permute(q, n_s)
    if aligned:
        small = jnp.concatenate([p[:, :, :128], p_other[:, :, :128]])
        tab_small = tab_p
    else:
        small = jnp.pad(small, ((0, 8 - small.shape[0]), (0, 0)))[None]
        for stage in (z, xy, core):
            small = spread(small, stage)
    taps, gain_in, gain_out, hp, skip_wide, meta, id_col, id_row = small_stage(tab_small, small, lines, n_dev, n_s, total)

    late = lax.all_gather(late, BOTH, axis=0, tiled=True).reshape(n_dev, 2, r_in, INNER)
    if not aligned:
        wg = late[:, 0].reshape(32, D // 32, INNER)
        wo = late[:, 1].reshape(n_dev, r_in, 2, D).transpose(0, 2, 1, 3).reshape(32, 2, D // 32, D)
        late = jnp.stack([wg, wo.transpose(0, 2, 1, 3).reshape(32, D // 32, INNER)], axis=1)

    def pieces(own, other, which):
        if aligned:
            return own, other, orders[which], lin[None]
        both = jnp.concatenate([own, other])[tables[which]]
        both = both.reshape(32, D // 32, both.shape[2])
        return both[:16], both[16:], np.arange(32), jnp.zeros((1,), jnp.int32)

    piece_p, piece_q = pieces(p, p_other, 0), pieces(q, q_other, 1)
    normed, conv_in, conv_pre, bc, x_part, dtx, hd, cumt, pay = first_stage(
        (halo, *got), gain_in, meta, taps, hp, piece_p, piece_q, total
    )

    def spans(k):
        return [d for d in range(n_s - k) if ((d + 1) * total - 1) // length == (d + k) * total // length]

    far = max(k for k in range(1, n_s) if spans(k))
    reaches = [1 << b for b in range(far.bit_length())]
    pay, normed, dtx, cumt, g = tied(pay, normed, dtx, cumt, g)
    forth = lambda v, k: lax.ppermute(v, "seq", [(d, d + k) for d in spans(k)])
    before = [forth(pay, k) for k in range(1, far + 1)]
    normed_p, normed_q = turn_stage(tab_p, tab_q, normed)
    inside = pairs_stage(bc, dtx, cumt, id_col, id_row, total)
    g = jnp.concatenate(g)
    ga, dga, gno = gate_stage(normed, g, late, total)
    inside, normed_p, normed_q, gno, *before = tied(inside, normed_p, normed_q, gno, *before)
    state_in, normed_out, e, grad_gate, pay_back, gc_state, row_sum, grad_gain_out = output_stage(
        before, inside, bc, x_part, hd, ga, dga, gno, gain_out, skip_wide, pay, total
    )

    back = lambda v, k: lax.ppermute(v, "seq", [(d + k, d) for d in spans(k)])
    adjoints = [back(pay_back, 1)]

    def sent(keep, send, which):
        if aligned:
            return keep, send
        both = jnp.concatenate([keep, send])
        both = both.reshape(n_dev, -1, both.shape[1])[jnp.asarray(orders[which]) ^ lin].reshape(both.shape)
        return both[: keep.shape[0]], both[keep.shape[0] :]

    ext_tok = jnp.concatenate([halo] + got)
    blocks = lambda v: v.reshape(n_dev // 2, -1, v.shape[1])
    keep_g, send_g, keep_o, send_o = weights_stage(tab_q, normed_p, grad_gate, normed_out, g, total)
    gdtx, gb_pairs, gc_pairs = pairs_back_stage(bc, dtx, e, cumt, id_col, id_row, total)
    rg, ro = sent(keep_g, send_g, 0), sent(keep_o, send_o, 1)
    (rg, ro), gdtx, gb_pairs, gc_pairs, normed_out, pay_back, *adjoints = tied((rg, ro), gdtx, gb_pairs, gc_pairs, normed_out, pay_back, *adjoints)
    held = pay_back
    for k in reaches[1:]:
        held = double_stage(held, adjoints[-1])
        adjoints.append(back(held, k))
    block_out, part = rest_stage(normed_out, grad_gate, ext_tok, late, total)
    rg, ro = fold_cut([blocks(v) for v in rg], core, y), fold_cut([blocks(v) for v in ro], core, x)
    (rg, ro), gdtx, block_out, part, *adjoints = tied((rg, ro), gdtx, block_out, part, *adjoints)

    conv_refs = (conv_pre, conv_in, taps, meta)
    head_refs = (gdtx, e, x_part, dtx, bc, state_in, hd, skip_wide)
    keep_q, send_q, proj_q, gt_q, acc, few = back_stage(adjoints, head_refs, conv_refs, normed_q, (), total)
    rg, ro = fold_cut(rg, y, x), fold_cut(ro, x, y)
    thirds = lambda v: [v[i * rows : (i + 1) * rows] for i in range(MB)]
    block_out = home(thirds(block_out))
    rq = sent(keep_q, send_q, 1)
    (rg, ro, rq), proj_q, gt_q, acc, few, block_out = tied((rg, ro, rq), proj_q, gt_q, acc, few, block_out)

    more = (acc, few, gc_state, gc_pairs, gb_pairs, row_sum, hp) + ((gt_q, grad_gain_out, tab_p) if aligned else ())
    keep_p, send_p, proj_p, gt_p, _, few = back_stage(
        adjoints, head_refs, conv_refs, normed_p, more, total, (n_dev, n_s) if aligned else ()
    )
    rg, ro = fold(rg, x), fold(ro, y)
    ro = jnp.concatenate([ro[:, : r_out // 2], ro[:, r_out // 2 :]], axis=2)
    both = cut(jnp.stack([rg, ro], axis=1), z)
    rp = sent(keep_p, send_p, 0)
    (both, rq, rp), proj_p, gt_p, few, block_out = tied((both, rq, rp), proj_p, gt_p, few, block_out)

    grad_normed = normed_stage(proj_p, proj_q, part, piece_p, piece_q)
    rp, rq = fold_cut([blocks(v) for v in rp], core, y), fold_cut([blocks(v) for v in rq], core, x)
    rim = lax.ppermute(grad_normed[:HALO], "seq", [(d + 1, d) for d in range(n_s - 1)])
    (rp, rq), grad_normed, rim = tied((rp, rq), grad_normed, rim)
    both = fold(both, z, F32)[0]
    rp, rq = fold_cut(rp, y, x), fold_cut(rq, x, y)
    grad_in = finish_stage(grad_normed, rim, ext_tok, g, gain_in, rows)
    (rp, rq), grad_in = tied((rp, rq), grad_in)
    grad_in = home(grad_in)
    w1_grad = cut(jnp.concatenate([fold(rp, x), fold(rq, y)], axis=2), z)
    w1_grad, both, block_out = tied(w1_grad, both, block_out)
    w1_grad = fold(w1_grad, z, F32)[0]
    if aligned:
        small = w1_grad[:8, H:128]
    else:
        small = grad_small_stage(tab_small, gt_p, gt_q, grad_gain_out, few, n_dev, n_s)
        for stage in (core, xy, z):
            small = fold(cut(small, stage), stage, F32)
        small = small[0]
    block_out, grad_in = placed(block_out), placed(grad_in)
    out_wo = jnp.concatenate([both[1, :, :D], both[1, :, D:]], axis=0)
    out_win = jnp.concatenate([both[0], w1_grad[:, FRONT:], w1_grad[:, 128:FRONT], w1_grad[:, :H]], axis=1)
    grad_gain = jnp.sum(out_win * w_in.astype(F32), axis=1) / norm_gain.astype(F32)
    count = dt_bias.shape[0]
    head = lambda k: small[7, k * count : (k + 1) * count]
    return (
        block_out, grad_in, grad_gain, out_win, small[:KERNEL, : conv_b.shape[0]], small[KERNEL, : conv_b.shape[0]],
        head(0), head(1), head(2), small[6, :r_out], out_wo,
    )


def solution(mesh):
    tok = P(None, "fsdp", "seq", None)
    row = P(None, "fsdp", None)
    specs = (tok, row, row, P(BOTH), P(BOTH, None), P(None, BOTH), P(BOTH), P("seq"), P("seq"), P("seq"), P(BOTH), P(BOTH, None), tok)
    outs = (tok, tok, P(BOTH), P(BOTH, None), P(None, BOTH), P(BOTH), P("seq"), P("seq"), P("seq"), P(BOTH), P(BOTH, None))
    return jax.shard_map(body, mesh=mesh, in_specs=specs, out_specs=outs, check_vma=False)
```
